32 devices in a mesh: inst: 8 (over z, y), tp: 4 (over x, core).
Axes of the slice: x: 2, y: 2, z: 4, core: 2. Of those that a mesh axis runs over, the one named last changes fastest.
Arguments:
- queries: bfloat16 [64, 3, 8192], P('inst', None, 'tp')
- new_kv: bfloat16 [64, 2, 3, 1024], P('inst', None, None, 'tp')
- key_value_pool: bfloat16 [960, 2, 64, 1024], P('inst', None, None, 'tp'), may hold values from -5 to 5
- ctx_len: int32 [64], P('inst'), may hold values from 257 to 960, as said below
- entry_lender: int32 [64, 5], P('inst'), may hold values from 0 to 7, as said below
- entry_blocks: int32 [64, 5], P('inst'), may hold values from 1 to 3
- entry_slot: int32 [64, 5], P('inst'), may hold values from 0 to 117, as said below
- out_weight: bfloat16 [8192, 4096], P('tp'), may hold values from -0.0625 to 0.0625
Outputs:
- attention: bfloat16 [64, 3, 8192], P('inst', None, 'tp')
- projected: bfloat16 [64, 3, 4096], P('inst', None, 'tp')
The draws below stay inside these ranges and needn't reach their ends.
Inputs may be any that keep to these rules, and one draw needn't show every extreme that they name: `ctx_len`: A request holds ((blocks of all its entries) - 1) * 64 + 1 to (blocks of all its entries) * 64 cached tokens. `entry_lender`: entry 0 is the request's home instance, the index of inst that holds its row; the other entries name other instances. The requests of one home name one other instance in at most 6 entries, and each instance is named by exactly 8 * (4) entries of other homes' requests. entry_slot + 3 <= 120; the blocks entry_slot to entry_slot + 2 of different entries on one instance never meet.
All inputs are finite; a program needn't handle non-finite values.
Results may differ from the reference program's by a relative error of at most 0.02.
Values may be sent and summed in bfloat16 or wider, within the bound.
A program may use at most 128 MiB of HBM per device.

```python
import math
import jax
import jax.numpy as jnp
from jax import lax

QUERY_HEADS = 64
KEY_VALUE_HEADS = 8
HEAD_SIZE = 128
DWIN = 4096
DECODE_STEPS = 3
BLOCK_TOKENS = 64
MOST_BLOCKS = 3
LEND = 5
REQ_DEV = 8
REQUEST_TOTAL = 64
POOL = 120
POOL_BLOCKS = 960
N_INST = 8


def block_plan(key):
    instances = N_INST
    lent_items = REQ_DEV * (LEND - 1)
    random_keys = jax.random.split(key, 6)
    placing = jax.random.permutation(random_keys[0], instances).astype(jnp.int32)
    inverse = jnp.argsort(placing).astype(jnp.int32)
    turning = jax.random.randint(random_keys[1], (), 0, instances - 1)
    homes = jnp.arange(instances, dtype=jnp.int32)[:, None]
    item_index = jnp.arange(lent_items, dtype=jnp.int32)[None, :]
    offsets = 1 + (item_index // 2 + turning) % (instances - 1)
    lender_item = inverse[(placing[homes] + offsets) % instances]
    groups = jax.vmap(lambda sub: jax.random.permutation(sub, REQ_DEV * LEND))(jax.random.split(random_keys[2], instances)).astype(jnp.int32)
    slot_item = groups[lender_item, REQ_DEV + item_index] * MOST_BLOCKS
    shuffled = jax.vmap(lambda sub: jax.random.permutation(sub, lent_items))(jax.random.split(random_keys[3], instances)).astype(jnp.int32)
    lender_far = jnp.take_along_axis(lender_item, shuffled, axis=1).reshape(instances, REQ_DEV, LEND - 1)
    slot_far = jnp.take_along_axis(slot_item, shuffled, axis=1).reshape(instances, REQ_DEV, LEND - 1)
    lenders = jnp.concatenate([jnp.broadcast_to(homes[:, :, None], (instances, REQ_DEV, 1)), lender_far], axis=2)
    slots = jnp.concatenate([(groups[:, :REQ_DEV] * MOST_BLOCKS)[:, :, None], slot_far], axis=2)
    blocks = jax.random.randint(random_keys[4], (instances, REQ_DEV, LEND), 1, MOST_BLOCKS + 1)
    blocks = blocks.at[:, 0, :].set(MOST_BLOCKS)
    blocks = blocks.at[1, 0, :].set(1)
    overall = jnp.sum(blocks, axis=2)
    length = BLOCK_TOKENS * (overall - 1) + jax.random.randint(random_keys[5], (instances, REQ_DEV), 1, BLOCK_TOKENS + 1)
    length = length.at[:, 0].set(BLOCK_TOKENS * overall[:, 0])
    length = length.at[1, 0].set(BLOCK_TOKENS * (LEND - 1) + 1)
    return (lenders.reshape(-1, LEND).astype(jnp.int32), blocks.reshape(-1, LEND).astype(jnp.int32), slots.reshape(-1, LEND).astype(jnp.int32), length.reshape(-1).astype(jnp.int32))


def fresh_keys(key):
    random_keys = jax.random.split(key, 3)
    base_random = jax.random.truncated_normal(random_keys[0], -4.0, 4.0, (REQUEST_TOTAL, DECODE_STEPS, KEY_VALUE_HEADS * HEAD_SIZE), jnp.float32)
    picked = jax.random.uniform(random_keys[2], (REQUEST_TOTAL,)) < 0.15
    moved = base_random[:, 1]
    second = jnp.where(picked[:, None], moved, base_random[:, 1])
    return base_random.at[:, 1].set(second)


def draw_ctx_len(key, part):
    return block_plan(key)[3]


def draw_entry_lender(key, part):
    return block_plan(key)[0]


def draw_entry_blocks(key, part):
    return block_plan(key)[1]


def draw_entry_slot(key, part):
    return block_plan(key)[2]


def draw_new_kv(key, part):
    local_keys = fresh_keys(key)
    key = jax.random.fold_in(key, 11)
    cached_values = jax.random.truncated_normal(key, -4.0, 4.0, (REQUEST_TOTAL, DECODE_STEPS, KEY_VALUE_HEADS * HEAD_SIZE), jnp.float32)
    return jnp.stack([local_keys, cached_values], axis=1).astype(jnp.bfloat16)


def draw_queries(key, part):
    local_keys = fresh_keys(key)
    key = jax.random.fold_in(key, 12)
    random_keys = jax.random.split(key, 3)
    expanded_heads = jnp.repeat(local_keys.reshape(REQUEST_TOTAL, DECODE_STEPS, KEY_VALUE_HEADS, 1, HEAD_SIZE), QUERY_HEADS // KEY_VALUE_HEADS, axis=3).reshape(REQUEST_TOTAL, DECODE_STEPS, QUERY_HEADS * HEAD_SIZE)
    result = 0.5 * expanded_heads + 0.9 * jax.random.truncated_normal(random_keys[2], -4.0, 4.0, expanded_heads.shape, jnp.float32)
    return result.astype(jnp.bfloat16)


def shard_levels(stream_key, extent, shards, least, largest):
    def one(position, parts):
        steps = jax.random.uniform(jax.random.fold_in(jax.random.fold_in(stream_key, 6), position), (parts,), jnp.float32, least / len(shards), largest / len(shards))
        return jnp.repeat(jnp.exp(steps), extent[position] // parts).reshape((-1,) + (1,) * (len(extent) - position - 1))

    gain = one(*shards[0])
    for cut in shards[1:]:
        gain = gain * one(*cut)
    return gain


def centred(stream_key, dims, scale, bound, pieces=(), held_as=jnp.bfloat16):
    values = scale * jax.random.normal(stream_key, dims, jnp.float32)
    if pieces:
        values = values * shard_levels(stream_key, dims, pieces, -0.22, 0.18)
    return jnp.clip(values, -bound, bound).astype(held_as)


def setup_inputs(seed: int = 0) -> dict:
    keys = jax.random.split(jax.random.key(seed), 9)
    return {
        "queries": draw_queries(jax.random.fold_in(keys[8], 71), 0),
        "new_kv": draw_new_kv(jax.random.fold_in(keys[8], 71), 0),
        "key_value_pool": centred(keys[2], (POOL_BLOCKS, 2, BLOCK_TOKENS, KEY_VALUE_HEADS * HEAD_SIZE), 1.0, 5.0, ((0, 8), (3, 4))),
        "ctx_len": draw_ctx_len(jax.random.fold_in(keys[8], 71), 0),
        "entry_lender": draw_entry_lender(jax.random.fold_in(keys[8], 71), 0),
        "entry_blocks": draw_entry_blocks(jax.random.fold_in(keys[8], 71), 0),
        "entry_slot": draw_entry_slot(jax.random.fold_in(keys[8], 71), 0),
        "out_weight": centred(keys[7], (QUERY_HEADS * HEAD_SIZE, DWIN), (QUERY_HEADS * HEAD_SIZE) ** -0.5, 0.0625, ((0, 4),)),
    }


def segment_attend(rows_of_queries, rows_of_keys, rows_of_values, visible):
    count_of_tokens = rows_of_keys.shape[0]
    head_groups = QUERY_HEADS // KEY_VALUE_HEADS
    heads_of_queries = rows_of_queries.astype(jnp.float32).reshape(DECODE_STEPS, KEY_VALUE_HEADS, head_groups, HEAD_SIZE)
    heads_of_keys = rows_of_keys.astype(jnp.float32).reshape(count_of_tokens, KEY_VALUE_HEADS, HEAD_SIZE)
    heads_of_values = rows_of_values.astype(jnp.float32).reshape(count_of_tokens, KEY_VALUE_HEADS, HEAD_SIZE)
    scores = jnp.einsum('sagd,tad->sagt', heads_of_queries, heads_of_keys, precision=lax.Precision.HIGHEST) * (1.0 / math.sqrt(HEAD_SIZE))
    scores = jnp.where(visible[:, None, None, :], scores, -1e+30)
    highest = lax.optimization_barrier(jnp.max(scores, axis=-1, keepdims=True))
    expits = jnp.exp(scores - highest)
    totals = lax.optimization_barrier(jnp.sum(expits, axis=-1, keepdims=True))
    logsum = (highest + jnp.log(totals))[..., 0].reshape(DECODE_STEPS, QUERY_HEADS)
    rounded = lax.optimization_barrier(expits.astype(jnp.bfloat16)).astype(jnp.float32)
    partial_out = jnp.einsum('sagt,tad->sagd', rounded, heads_of_values, precision=lax.Precision.HIGHEST) / totals
    return (partial_out.reshape(DECODE_STEPS, QUERY_HEADS * HEAD_SIZE).astype(jnp.bfloat16), logsum)

def request_attention(packed, key_value_pool):
    rows_of_queries, fresh, length, lenders, blocks, slots = packed
    positions = jnp.arange(MOST_BLOCKS * BLOCK_TOKENS, dtype=jnp.int32)
    earlier = jnp.cumsum(blocks) - blocks
    causal = jnp.arange(DECODE_STEPS)[None, :] <= jnp.arange(DECODE_STEPS)[:, None]
    partials = []
    logsums = []
    for entry_index in range(LEND):
        block_ids = (lenders[entry_index] * POOL + slots[entry_index] + jnp.arange(MOST_BLOCKS, dtype=jnp.int32)).astype(jnp.int32)
        selected_entries = key_value_pool[block_ids]
        rows_of_keys = selected_entries[:, 0].reshape(MOST_BLOCKS * BLOCK_TOKENS, KEY_VALUE_HEADS * HEAD_SIZE)
        rows_of_values = selected_entries[:, 1].reshape(MOST_BLOCKS * BLOCK_TOKENS, KEY_VALUE_HEADS * HEAD_SIZE)
        live_count = jnp.clip(length - BLOCK_TOKENS * earlier[entry_index], 0, BLOCK_TOKENS * blocks[entry_index])
        visible = jnp.broadcast_to(positions[None, :] < live_count, (DECODE_STEPS, MOST_BLOCKS * BLOCK_TOKENS))
        if entry_index == 0:
            rows_of_keys = jnp.concatenate([rows_of_keys, fresh[0]], axis=0)
            rows_of_values = jnp.concatenate([rows_of_values, fresh[1]], axis=0)
            visible = jnp.concatenate([visible, causal], axis=1)
        partial_out, logsum = segment_attend(rows_of_queries, rows_of_keys, rows_of_values, visible)
        partials.append(partial_out)
        logsums.append(logsum)
    logsums = jnp.stack(logsums)
    partials = jnp.stack(partials).astype(jnp.float32).reshape(LEND, DECODE_STEPS, QUERY_HEADS, HEAD_SIZE)
    highest = lax.optimization_barrier(jnp.max(logsums, axis=0, keepdims=True))
    weights = jnp.exp(logsums - highest)
    merged = lax.optimization_barrier(jnp.sum(weights[..., None] * partials, axis=0)) / lax.optimization_barrier(jnp.sum(weights, axis=0))[..., None]
    return merged.reshape(DECODE_STEPS, QUERY_HEADS * HEAD_SIZE).astype(jnp.bfloat16)

def reference(queries, new_kv, key_value_pool, ctx_len, entry_lender, entry_blocks, entry_slot, out_weight):
    attention = lax.map(lambda packed: request_attention(packed, key_value_pool), (queries, new_kv, ctx_len, entry_lender, entry_blocks, entry_slot))
    flat = attention.reshape(REQUEST_TOTAL * DECODE_STEPS, QUERY_HEADS * HEAD_SIZE)
    projected = jnp.dot(flat, out_weight, preferred_element_type=jnp.float32).astype(jnp.bfloat16)
    return (attention, projected.reshape(REQUEST_TOTAL, DECODE_STEPS, DWIN))
```

```python
import functools
import math

import jax
import jax.numpy as jnp
from jax import lax
from jax.experimental import pallas as pl
from jax.experimental.pallas import tpu as pltpu
from jax.sharding import PartitionSpec as P

HEAD_SIZE = 128
GROUP = 8
MOST_BLOCKS = 3
MESH = pl.DeviceIdType.MESH
SCALE = 1.0 / math.sqrt(HEAD_SIZE)


def attend(q, keys, values, seen, kv_heads):
    rows = q.shape[0]
    per = rows // kv_heads
    if kv_heads > 1:
        wide = jnp.concatenate([q] * kv_heads, axis=1)
        r = lax.broadcasted_iota(jnp.int32, wide.shape, 0) // per
        c = lax.broadcasted_iota(jnp.int32, wide.shape, 1) // HEAD_SIZE
        wide = jnp.where(r == c, wide.astype(jnp.float32), 0.0).astype(jnp.bfloat16)
    else:
        wide = q
    s = lax.dot_general(wide, keys, (((1,), (1,)), ((), ())), preferred_element_type=jnp.float32) * SCALE
    s = jnp.where(seen, s, -1e30)
    top = jnp.max(s, axis=1, keepdims=True)
    e = jnp.exp(s - top)
    total = jnp.sum(e, axis=1, keepdims=True)
    o = jnp.dot(e.astype(jnp.bfloat16), values, preferred_element_type=jnp.float32)
    if kv_heads > 1:
        o = jnp.concatenate(
            [o[a * per : (a + 1) * per, a * HEAD_SIZE : (a + 1) * HEAD_SIZE] for a in range(kv_heads)], axis=0
        )
    return o * (1.0 / total), top + jnp.log(total)


def to_rows(columns):
    pad = jnp.zeros((128 - columns.shape[0], 128), columns.dtype)
    return jnp.transpose(jnp.concatenate([columns, pad], axis=0))


def kernel(
    dims,
    info, q_ref, meta_ref, new_ref, pool_hbm, weight_hbm,
    att_ref, proj_ref,
    pool, weight, send_q, got_q, got_meta, live_smem, send_part, got_part, send_lse, got_lse,
    home_part, spread, attn, send_y, got_y,
    pool_sem, weight_sem, q_send, q_recv, m_send, m_recv, smem_sem, p_send, p_recv, l_send, l_recv, y_send, y_recv,
):
    n, tps, cap, requests, steps, kv, entries = dims
    rows = kv * steps * GROUP
    span = MOST_BLOCKS * pool.shape[2]
    me = lax.axis_index("inst")
    tp = lax.axis_index("tp")
    chunk = weight.shape[2]

    pool_parts = pool_sem.shape[0]
    part = pool.shape[0] // pool_parts
    pool_copies = [
        pltpu.make_async_copy(pool_hbm.at[pl.ds(i * part, part)], pool.at[pl.ds(i * part, part)], pool_sem.at[i])
        for i in range(pool_parts)
    ]
    for copy in pool_copies:
        copy.start()
    order = [tps // 2] + [o for o in range(1, tps) if o != tps // 2] + [0]
    weight_copies = {}
    for o in order:
        col = pl.multiple_of(((tp + o) % tps) * chunk, chunk)
        weight_copies[o] = pltpu.make_async_copy(weight_hbm.at[:, pl.ds(col, chunk)], weight.at[o], weight_sem.at[o])
        weight_copies[o].start()

    barrier = pltpu.get_barrier_semaphore()
    for j in range(1, n):
        pl.semaphore_signal(barrier, inc=1, device_id=((me + j) % n, tp), device_id_type=MESH)
    for o in range(1, tps):
        pl.semaphore_signal(barrier, inc=1, device_id=(me, (tp + o) % tps), device_id_type=MESH)

    base = requests + requests * (entries - 1)
    for j in range(1, n):
        for k in range(cap):
            code = info[base + j * cap + k]
            send_q[j, k] = q_ref[lax.shift_right_logical(code, 16)]
    pl.semaphore_wait(barrier, n - 1 + tps - 1)

    def q_copy(j):
        return pltpu.make_async_remote_copy(
            src_ref=send_q.at[j], dst_ref=got_q.at[j], send_sem=q_send.at[j], recv_sem=q_recv.at[j],
            device_id=((me + j) % n, tp), device_id_type=MESH,
        )

    def m_copy(j):
        return pltpu.make_async_remote_copy(
            src_ref=meta_ref.at[j], dst_ref=got_meta.at[j], send_sem=m_send.at[j], recv_sem=m_recv.at[j],
            device_id=((me + j) % n, tp), device_id_type=MESH,
        )

    def p_copy(j):
        return pltpu.make_async_remote_copy(
            src_ref=send_part.at[j], dst_ref=got_part.at[j], send_sem=p_send.at[j], recv_sem=p_recv.at[j],
            device_id=((me + n - j) % n, tp), device_id_type=MESH,
        )

    def l_copy(j):
        return pltpu.make_async_remote_copy(
            src_ref=send_lse.at[j], dst_ref=got_lse.at[j], send_sem=l_send.at[j], recv_sem=l_recv.at[j],
            device_id=((me + n - j) % n, tp), device_id_type=MESH,
        )

    for j in range(1, n):
        m_copy(j).start()
    for j in range(1, n):
        q_copy(j).start()
    for copy in pool_copies:
        copy.wait()

    def fetch(group):
        taken = pool[pl.ds(group * MOST_BLOCKS, MOST_BLOCKS)]
        return taken[:, 0].reshape(span, kv * HEAD_SIZE), taken[:, 1].reshape(span, kv * HEAD_SIZE)

    lane = lax.broadcasted_iota(jnp.int32, (rows, 128), 1)
    fresh = new_ref.shape[2]
    home_col = lax.broadcasted_iota(jnp.int32, (rows, span + fresh), 1)
    home_step = (lax.broadcasted_iota(jnp.int32, (rows, span + fresh), 0) // GROUP) % steps
    own_seen = (home_col >= span) & (home_col - span <= home_step)

    def home_step_fn(i, columns):
        for u in range(requests // 2):
            r = i * (requests // 2) + u
            code = info[r]
            keys, values = fetch(lax.shift_right_logical(code, 8) & 255)
            keys = jnp.concatenate([keys, new_ref[r, 0]], axis=0)
            values = jnp.concatenate([values, new_ref[r, 1]], axis=0)
            seen = (home_col < jnp.minimum(code & 255, span)) | own_seen
            o, lse = attend(q_ref[r], keys, values, seen, kv)
            home_part[r] = o.astype(jnp.bfloat16)
            columns = jnp.where(lane == r, lse, columns)
        return columns

    home_columns = lax.fori_loop(0, 2, home_step_fn, jnp.zeros((rows, 128), jnp.float32))
    home_lse = to_rows(home_columns)[:requests]

    lent_col = lax.broadcasted_iota(jnp.int32, (rows, span), 1)

    def lend(j, carry):
        m_copy(j).wait_recv()
        down = pltpu.make_async_copy(got_meta.at[j], live_smem.at[j], smem_sem.at[j])
        down.start()
        q_copy(j).wait_recv()
        down.wait()
        columns = jnp.zeros((rows, 128), jnp.float32)
        for k in range(cap):
            code = live_smem[j, 0, k]
            keys, values = fetch(lax.shift_right_logical(code, 8) & 255)
            q = got_q[j, k]
            o, lse = attend(q, keys, values, lent_col < (code & 255), kv)
            send_part[j, k] = o.astype(jnp.bfloat16)
            columns = jnp.where(lane == k, lse, columns)
        send_lse[j] = to_rows(columns)[:8]
        p_copy(j).start()
        l_copy(j).start()
        return carry

    lax.fori_loop(1, n, lend, 0)

    for j in range(1, n):
        l_copy(j).wait_recv()
    logsums = [home_lse]
    for e in range(1, entries):
        picked = []
        for r in range(requests):
            where = info[requests + r * (entries - 1) + e - 1]
            at = lax.shift_right_logical(where, 8)
            picked.append(got_lse[at, pl.ds(where & 255, 1), :])
        logsums.append(jnp.concatenate(picked, axis=0))
    highest = functools.reduce(jnp.maximum, logsums)
    weights = [jnp.exp(x - highest) for x in logsums]
    inverse = 1.0 / functools.reduce(jnp.add, weights)
    stacked = jnp.concatenate([w * inverse for w in weights], axis=0)
    stacked = jnp.concatenate([stacked, jnp.zeros((128 - stacked.shape[0], 128), jnp.float32)], axis=0)
    by_head = jnp.transpose(stacked)[:rows]

    for j in range(1, n):
        p_copy(j).wait_recv()
    per = steps * GROUP
    for r in range(requests):
        total = by_head[:, r : r + 1] * home_part[r].astype(jnp.float32)
        for e in range(1, entries):
            where = info[requests + r * (entries - 1) + e - 1]
            at = lax.shift_right_logical(where, 8)
            rank = where & 255
            far = got_part[at, rank]
            c = e * requests + r
            total = total + by_head[:, c : c + 1] * far.astype(jnp.float32)
        for a in range(kv):
            spread[(a * requests + r) * per : (a * requests + r + 1) * per, :] = total[a * per : (a + 1) * per]
    tokens = requests * steps
    for a in range(kv):
        for g in range(GROUP):
            block = spread[pl.ds(a * requests * per + g, tokens, stride=GROUP), :]
            h = a * GROUP + g
            attn[:, h * HEAD_SIZE : (h + 1) * HEAD_SIZE] = block.astype(jnp.bfloat16)
    att_ref[...] = attn[...]

    def y_copy(o):
        return pltpu.make_async_remote_copy(
            src_ref=send_y.at[o], dst_ref=got_y.at[o], send_sem=y_send.at[o], recv_sem=y_recv.at[o],
            device_id=(me, (tp + o) % tps), device_id_type=MESH,
        )

    half = chunk // 2
    own = None
    for o in order:
        weight_copies[o].wait()
        y = jnp.dot(attn[...], weight[o], preferred_element_type=jnp.float32)
        y = jnp.concatenate([y[:, :half], y[:, half:]], axis=0)
        if o == 0:
            own = y
        else:
            send_y[o] = y.astype(jnp.bfloat16)
            y_copy(o).start()
    for o in order[:-1]:
        y_copy(o).wait_recv()
        own = own + got_y[o].astype(jnp.float32)
    proj_ref[:, :half] = own[:tokens].astype(jnp.bfloat16)
    proj_ref[:, half:] = own[tokens:].astype(jnp.bfloat16)

    for j in range(1, n):
        m_copy(j).wait_send()
        q_copy(j).wait_send()
        p_copy(j).wait_send()
        l_copy(j).wait_send()
    for o in range(1, tps):
        y_copy(o).wait_send()


def local(queries, new_kv, key_value_pool, ctx_len, entry_lender, entry_blocks, entry_slot, out_weight):
    requests, steps, query_width = queries.shape
    heads = query_width // HEAD_SIZE
    kv = key_value_pool.shape[3] // HEAD_SIZE
    entries = entry_lender.shape[1]
    n = lax.axis_size("inst")
    tps = lax.axis_size("tp")
    me = lax.axis_index("inst")
    block_rows = key_value_pool.shape[2]
    items = requests * (entries - 1)
    cap = 2 * ((items // 2 + n - 2) // (n - 1))
    rows = heads * steps
    span = MOST_BLOCKS * block_rows

    e_index = jnp.arange(entries)
    before = jnp.sum(jnp.where(e_index[None, :, None] > e_index[None, None, :], entry_blocks[:, None, :], 0), axis=2)
    live = jnp.clip(ctx_len[:, None] - block_rows * before, 0, block_rows * entry_blocks)
    group = entry_slot // MOST_BLOCKS
    code = (jnp.arange(requests)[:, None] * 65536 + group * 256 + live).astype(jnp.int32)
    offset = ((entry_lender[:, 1:] - me + n) % n).reshape(items)
    order = jnp.arange(items)
    rank = jnp.sum(
        ((offset[:, None] == offset[None, :]) & (order[None, :] < order[:, None])).astype(jnp.int32), axis=1
    )
    place = offset * cap + rank
    table = jnp.sum(
        jnp.where(place[None, :] == jnp.arange(n * cap)[:, None], code[:, 1:].reshape(1, items), 0), axis=1
    )
    info = jnp.concatenate([code[:, 0] & 65535, offset * 256 + rank, table]).astype(jnp.int32)
    meta = jnp.pad(table.reshape(n, 1, cap), ((0, 0), (0, 7), (0, 128 - cap))).astype(jnp.int32)

    q = queries.reshape(requests, steps, kv, GROUP, HEAD_SIZE).transpose(0, 2, 1, 3, 4)
    q = q.reshape(requests, rows, HEAD_SIZE)
    fresh = jnp.pad(new_kv, ((0, 0), (0, 0), (0, 16 - steps), (0, 0)))

    tokens = requests * steps
    chunk = out_weight.shape[1] // tps
    vmem = pl.BlockSpec(memory_space=pltpu.VMEM)
    hbm = pl.BlockSpec(memory_space=pl.ANY)
    bf, f32 = jnp.bfloat16, jnp.float32
    dma = pltpu.SemaphoreType.DMA
    att, proj = pl.pallas_call(
        functools.partial(kernel, (n, tps, cap, requests, steps, kv, entries)),
        out_shape=(
            jax.ShapeDtypeStruct((tokens, query_width), bf),
            jax.ShapeDtypeStruct((tokens, chunk), bf),
        ),
        in_specs=[pl.BlockSpec(memory_space=pltpu.SMEM), vmem, vmem, vmem, hbm, hbm],
        out_specs=(vmem, vmem),
        scratch_shapes=[
            pltpu.VMEM(key_value_pool.shape, bf),
            pltpu.VMEM((tps, out_weight.shape[0], chunk), bf),
            pltpu.VMEM((n, cap, rows, HEAD_SIZE), bf),
            pltpu.VMEM((n, cap, rows, HEAD_SIZE), bf),
            pltpu.VMEM((n, 8, 128), jnp.int32),
            pltpu.SMEM((n, 8, 128), jnp.int32),
            pltpu.VMEM((n, cap, rows, HEAD_SIZE), bf),
            pltpu.VMEM((n, cap, rows, HEAD_SIZE), bf),
            pltpu.VMEM((n, 8, 128), f32),
            pltpu.VMEM((n, 8, 128), f32),
            pltpu.VMEM((requests, rows, HEAD_SIZE), bf),
            pltpu.VMEM((requests * rows, HEAD_SIZE), f32),
            pltpu.VMEM((tokens, query_width), bf),
            pltpu.VMEM((tps, 2 * tokens, chunk // 2), bf),
            pltpu.VMEM((tps, 2 * tokens, chunk // 2), bf),
            dma((4,)), dma((tps,)),
            dma((n,)), dma((n,)), dma((n,)), dma((n,)), dma((n,)),
            dma((n,)), dma((n,)), dma((n,)), dma((n,)),
            dma((tps,)), dma((tps,)),
        ],
        compiler_params=pltpu.CompilerParams(
            collective_id=0, has_side_effects=True, vmem_limit_bytes=52 * 1024 * 1024
        ),
    )(info, q, meta, fresh, key_value_pool, out_weight)
    return att.reshape(requests, steps, query_width), proj.reshape(requests, steps, chunk)


def solution(mesh):
    return jax.shard_map(
        local,
        mesh=mesh,
        in_specs=(
            P("inst", None, "tp"),
            P("inst", None, None, "tp"),
            P("inst", None, None, "tp"),
            P("inst"),
            P("inst", None),
            P("inst", None),
            P("inst", None),
            P("tp", None),
        ),
        out_specs=(P("inst", None, "tp"), P("inst", None, "tp")),
        check_vma=False,
    )
```

```python
import functools
import math

import jax
import jax.numpy as jnp
from jax import lax
from jax.experimental import pallas as pl
from jax.experimental.pallas import tpu as pltpu
from jax.sharding import PartitionSpec as P

HEAD_SIZE = 128
GROUP = 8
MOST_BLOCKS = 3
MESH = pl.DeviceIdType.MESH
SCALE = 1.0 / math.sqrt(HEAD_SIZE)


def attend(q, keys, values, seen, kv_heads):
    rows = q.shape[0]
    per = rows // kv_heads
    if kv_heads > 1:
        wide = jnp.concatenate([q] * kv_heads, axis=1)
        r = lax.broadcasted_iota(jnp.int32, wide.shape, 0) // per
        c = lax.broadcasted_iota(jnp.int32, wide.shape, 1) // HEAD_SIZE
        wide = jnp.where(r == c, wide.astype(jnp.float32), 0.0).astype(jnp.bfloat16)
    else:
        wide = q
    s = lax.dot_general(wide, keys, (((1,), (1,)), ((), ())), preferred_element_type=jnp.float32) * SCALE
    s = jnp.where(seen, s, -1e30)
    top = jnp.max(s, axis=1, keepdims=True)
    e = jnp.exp(s - top)
    total = jnp.sum(e, axis=1, keepdims=True)
    o = jnp.dot(e.astype(jnp.bfloat16), values, preferred_element_type=jnp.float32)
    if kv_heads > 1:
        o = jnp.concatenate(
            [o[a * per : (a + 1) * per, a * HEAD_SIZE : (a + 1) * HEAD_SIZE] for a in range(kv_heads)], axis=0
        )
    return o * (1.0 / total), top + jnp.log(total)


def to_rows(columns):
    pad = jnp.zeros((128 - columns.shape[0], 128), columns.dtype)
    return jnp.transpose(jnp.concatenate([columns, pad], axis=0))


def kernel(
    dims,
    ctx_ref, lender_ref, blocks_ref, slot_ref, q_ref, new_ref, pool_hbm, weight_hbm,
    att_ref, proj_ref,
    pool, weight, send_q, got_q, send_meta, got_meta, live_smem, plan_vmem, plan, send_part, got_part, send_lse,
    got_lse, home_part, spread, attn, send_y, got_y, queries, fresh_rows,
    pool_sem, weight_sem, q_send, q_recv, m_send, m_recv, smem_sem, p_send, p_recv, l_send, l_recv, y_send, y_recv,
    plan_sem,
):
    n, tps, cap, requests, steps, kv, entries = dims
    rows = kv * steps * GROUP
    block_rows = pool.shape[2]
    span = MOST_BLOCKS * block_rows
    me = lax.axis_index("inst")
    tp = lax.axis_index("tp")
    chunk = weight.shape[2]
    offsets = [n // 2 + ((i + 1) // 2) * (1 - 2 * (i % 2)) for i in range(n - 1)]

    barrier = pltpu.get_barrier_semaphore()
    for j in range(1, n):
        pl.semaphore_signal(barrier, inc=1, device_id=((me + j) % n, tp), device_id_type=MESH)
    for o in range(1, tps):
        pl.semaphore_signal(barrier, inc=1, device_id=(me, (tp + o) % tps), device_id_type=MESH)

    pool_parts = pool_sem.shape[0]
    part = pool.shape[0] // pool_parts
    pool_copies = [
        pltpu.make_async_copy(pool_hbm.at[pl.ds(i * part, part)], pool.at[pl.ds(i * part, part)], pool_sem.at[i])
        for i in range(pool_parts)
    ]
    for copy in pool_copies:
        copy.start()
    order = [tps // 2] + [o for o in range(1, tps) if o != tps // 2] + [0]
    weight_copies = {}
    for o in order:
        col = pl.multiple_of(((tp + o) % tps) * chunk, chunk)
        weight_copies[o] = pltpu.make_async_copy(weight_hbm.at[:, pl.ds(col, chunk)], weight.at[o], weight_sem.at[o])
        weight_copies[o].start()

    plan_row = lax.broadcasted_iota(jnp.int32, (n, 128), 0)
    plan_lane = lax.broadcasted_iota(jnp.int32, (n, 128), 1)
    table = jnp.zeros((n, 128), jnp.int32)
    used = jnp.zeros((n, 128), jnp.int32)
    ranks = jnp.zeros((n, 128), jnp.int32)
    home_codes, entry_offsets = [], []
    for r in range(requests):
        before = 0
        for e in range(entries):
            blocks = blocks_ref[r, e]
            live = jnp.clip(ctx_ref[r] - block_rows * before, 0, block_rows * blocks)
            before = before + blocks
            group = lax.div(slot_ref[r, e], MOST_BLOCKS)
            if e == 0:
                home_codes.append((group, live))
                continue
            away = lender_ref[r, e] - me
            away = jnp.where(away < 0, away + n, away)
            entry_offsets.append(away)
            code = r * 65536 + group * 256 + live
            hit = plan_row == away
            table = jnp.where(hit & (plan_lane == used), code, table)
            ranks = jnp.where(hit & (plan_lane == len(entry_offsets) - 1), jnp.minimum(used, cap - 1), ranks)
            used = used + jnp.where(hit, 1, 0)
    plan_vmem[0:n] = table
    plan_vmem[n : n + 8] = jnp.broadcast_to(jnp.sum(ranks, axis=0, keepdims=True), (8, 128))
    plan_copy = pltpu.make_async_copy(plan_vmem, plan, plan_sem)
    plan_copy.start()
    for j in range(1, n):
        send_meta[j] = jnp.broadcast_to(table[j : j + 1], (8, 128))

    for s in range(steps):
        for h in range(kv * GROUP):
            a, g = h // GROUP, h % GROUP
            block = q_ref[s, :, h * HEAD_SIZE : (h + 1) * HEAD_SIZE].astype(jnp.float32)
            spread[pl.ds((a * steps + s) * GROUP + g, requests, stride=rows), :] = block
    for r in range(requests):
        queries[r] = spread[r * rows : (r + 1) * rows, :].astype(jnp.bfloat16)

    plan_copy.wait()
    for j in offsets:
        for k in range(cap):
            send_q[j, k] = queries[lax.shift_right_logical(plan[j, k], 16)]
    pl.semaphore_wait(barrier, n - 1 + tps - 1)

    def q_copy(j):
        return pltpu.make_async_remote_copy(
            src_ref=send_q.at[j], dst_ref=got_q.at[j], send_sem=q_send.at[j], recv_sem=q_recv.at[j],
            device_id=((me + j) % n, tp), device_id_type=MESH,
        )

    def m_copy(j):
        return pltpu.make_async_remote_copy(
            src_ref=send_meta.at[j], dst_ref=got_meta.at[j], send_sem=m_send.at[j], recv_sem=m_recv.at[j],
            device_id=((me + j) % n, tp), device_id_type=MESH,
        )

    def p_copy(j):
        return pltpu.make_async_remote_copy(
            src_ref=send_part.at[j], dst_ref=got_part.at[j], send_sem=p_send.at[j], recv_sem=p_recv.at[j],
            device_id=((me + n - j) % n, tp), device_id_type=MESH,
        )

    def l_copy(j):
        return pltpu.make_async_remote_copy(
            src_ref=send_lse.at[j], dst_ref=got_lse.at[j], send_sem=l_send.at[j], recv_sem=l_recv.at[j],
            device_id=((me + n - j) % n, tp), device_id_type=MESH,
        )

    for j in offsets:
        m_copy(j).start()
        q_copy(j).start()
    fresh_rows[...] = jnp.zeros_like(fresh_rows)
    for r in range(requests):
        for i in range(steps):
            pair = new_ref[r, i].astype(jnp.float32)
            for c in range(2):
                fresh_rows[r, c, i : i + 1, :] = pair[c : c + 1]
    for copy in pool_copies:
        copy.wait()

    def fetch(group):
        taken = pool[pl.ds(group * MOST_BLOCKS, MOST_BLOCKS)]
        return taken[:, 0].reshape(span, kv * HEAD_SIZE), taken[:, 1].reshape(span, kv * HEAD_SIZE)

    lane = lax.broadcasted_iota(jnp.int32, (rows, 128), 1)
    fresh = fresh_rows.shape[2]
    home_col = lax.broadcasted_iota(jnp.int32, (rows, span + fresh), 1)
    home_step = (lax.broadcasted_iota(jnp.int32, (rows, span + fresh), 0) // GROUP) % steps
    own_seen = (home_col >= span) & (home_col - span <= home_step)

    home_columns = jnp.zeros((rows, 128), jnp.float32)
    for r in range(requests):
        group, live = home_codes[r]
        keys, values = fetch(group)
        keys = jnp.concatenate([keys, fresh_rows[r, 0].astype(jnp.bfloat16)], axis=0)
        values = jnp.concatenate([values, fresh_rows[r, 1].astype(jnp.bfloat16)], axis=0)
        o, lse = attend(queries[r], keys, values, (home_col < live) | own_seen, kv)
        home_part[r] = o.astype(jnp.bfloat16)
        home_columns = jnp.where(lane == r, lse, home_columns)
    home_lse = to_rows(home_columns)[:requests]

    lent_col = lax.broadcasted_iota(jnp.int32, (rows, span), 1)

    def lend(i, carry):
        j = n // 2 + ((i + 1) // 2) * (1 - 2 * (i % 2))
        m_copy(j).wait_recv()
        down = pltpu.make_async_copy(got_meta.at[j], live_smem.at[j], smem_sem.at[j])
        down.start()
        q_copy(j).wait_recv()
        down.wait()
        columns = jnp.zeros((rows, 128), jnp.float32)
        for k in range(cap):
            code = live_smem[j, 0, k]
            keys, values = fetch(lax.shift_right_logical(code, 8) & 255)
            q = got_q[j, k]
            o, lse = attend(q, keys, values, lent_col < (code & 255), kv)
            send_part[j, k] = o.astype(jnp.bfloat16)
            columns = jnp.where(lane == k, lse, columns)
        send_lse[j] = to_rows(columns)[:8]
        p_copy(j).start()
        l_copy(j).start()
        return carry

    lax.fori_loop(0, n - 1, lend, 0)

    for j in range(1, n):
        l_copy(j).wait_recv()
    logsums = [home_lse]
    for e in range(1, entries):
        picked = []
        for r in range(requests):
            item = r * (entries - 1) + e - 1
            picked.append(got_lse[entry_offsets[item], pl.ds(plan[n, item], 1), :])
        logsums.append(jnp.concatenate(picked, axis=0))
    highest = functools.reduce(jnp.maximum, logsums)
    weights = [jnp.exp(x - highest) for x in logsums]
    inverse = 1.0 / functools.reduce(jnp.add, weights)
    stacked = jnp.concatenate([w * inverse for w in weights], axis=0)
    stacked = jnp.concatenate([stacked, jnp.zeros((128 - stacked.shape[0], 128), jnp.float32)], axis=0)
    by_head = jnp.transpose(stacked)[:rows]

    for j in range(1, n):
        p_copy(j).wait_recv()
    for r in range(requests):
        total = by_head[:, r : r + 1] * home_part[r].astype(jnp.float32)
        for e in range(1, entries):
            item = r * (entries - 1) + e - 1
            far = got_part[entry_offsets[item], plan[n, item]]
            c = e * requests + r
            total = total + by_head[:, c : c + 1] * far.astype(jnp.float32)
        spread[r * rows : (r + 1) * rows, :] = total
    tokens = requests * steps
    for h in range(kv * GROUP):
        a, g = h // GROUP, h % GROUP
        block = jnp.concatenate(
            [spread[pl.ds((a * steps + s) * GROUP + g, requests, stride=rows), :] for s in range(steps)], axis=0
        )
        attn[:, h * HEAD_SIZE : (h + 1) * HEAD_SIZE] = block.astype(jnp.bfloat16)
        for s in range(steps):
            att_ref[s, :, h * HEAD_SIZE : (h + 1) * HEAD_SIZE] = block[s * requests : (s + 1) * requests].astype(
                jnp.bfloat16
            )

    def y_copy(o):
        return pltpu.make_async_remote_copy(
            src_ref=send_y.at[o], dst_ref=got_y.at[o], send_sem=y_send.at[o], recv_sem=y_recv.at[o],
            device_id=(me, (tp + o) % tps), device_id_type=MESH,
        )

    half = chunk // 2
    own = None
    for o in order:
        weight_copies[o].wait()
        y = jnp.dot(attn[...], weight[o], preferred_element_type=jnp.float32)
        y = jnp.concatenate([y[:, :half], y[:, half:]], axis=0)
        if o == 0:
            own = y
        else:
            send_y[o] = y.astype(jnp.bfloat16)
            y_copy(o).start()
    for o in order[:-1]:
        y_copy(o).wait_recv()
        own = own + got_y[o].astype(jnp.float32)
    for s in range(steps):
        proj_ref[s, :, :half] = own[s * requests : (s + 1) * requests].astype(jnp.bfloat16)
        proj_ref[s, :, half:] = own[tokens + s * requests : tokens + (s + 1) * requests].astype(jnp.bfloat16)

    for j in range(1, n):
        m_copy(j).wait_send()
        q_copy(j).wait_send()
        p_copy(j).wait_send()
        l_copy(j).wait_send()
    for o in range(1, tps):
        y_copy(o).wait_send()


def local(queries, new_kv, key_value_pool, ctx_len, entry_lender, entry_blocks, entry_slot, out_weight):
    requests, steps, query_width = queries.shape
    heads = query_width // HEAD_SIZE
    kv = key_value_pool.shape[3] // HEAD_SIZE
    entries = entry_lender.shape[1]
    n = lax.axis_size("inst")
    tps = lax.axis_size("tp")
    items = requests * (entries - 1)
    cap = 2 * ((items // 2 + n - 2) // (n - 1))
    rows = heads * steps

    tokens = requests * steps
    chunk = out_weight.shape[1] // tps
    vmem = pl.BlockSpec(memory_space=pltpu.VMEM)
    hbm = pl.BlockSpec(memory_space=pl.ANY)
    bf, f32 = jnp.bfloat16, jnp.float32
    dma = pltpu.SemaphoreType.DMA
    att, proj = pl.pallas_call(
        functools.partial(kernel, (n, tps, cap, requests, steps, kv, entries)),
        out_shape=(
            jax.ShapeDtypeStruct((steps, requests, query_width), bf),
            jax.ShapeDtypeStruct((steps, requests, chunk), bf),
        ),
        in_specs=[pl.BlockSpec(memory_space=pltpu.SMEM)] * 4 + [vmem, vmem, hbm, hbm],
        out_specs=(vmem, vmem),
        scratch_shapes=[
            pltpu.VMEM(key_value_pool.shape, bf),
            pltpu.VMEM((tps, out_weight.shape[0], chunk), bf),
            pltpu.VMEM((n, cap, rows, HEAD_SIZE), bf),
            pltpu.VMEM((n, cap, rows, HEAD_SIZE), bf),
            pltpu.VMEM((n, 8, 128), jnp.int32),
            pltpu.VMEM((n, 8, 128), jnp.int32),
            pltpu.SMEM((n, 8, 128), jnp.int32),
            pltpu.VMEM((n + 8, 128), jnp.int32),
            pltpu.SMEM((n + 8, 128), jnp.int32),
            pltpu.VMEM((n, cap, rows, HEAD_SIZE), bf),
            pltpu.VMEM((n, cap, rows, HEAD_SIZE), bf),
            pltpu.VMEM((n, 8, 128), f32),
            pltpu.VMEM((n, 8, 128), f32),
            pltpu.VMEM((requests, rows, HEAD_SIZE), bf),
            pltpu.VMEM((requests * rows, HEAD_SIZE), f32),
            pltpu.VMEM((tokens, query_width), bf),
            pltpu.VMEM((tps, 2 * tokens, chunk // 2), bf),
            pltpu.VMEM((tps, 2 * tokens, chunk // 2), bf),
            pltpu.VMEM((requests, rows, HEAD_SIZE), bf),
            pltpu.VMEM((requests, 2, 16, key_value_pool.shape[3]), f32),
            dma((4,)), dma((tps,)),
            dma((n,)), dma((n,)), dma((n,)), dma((n,)), dma((n,)),
            dma((n,)), dma((n,)), dma((n,)), dma((n,)),
            dma((tps,)), dma((tps,)), dma,
        ],
        compiler_params=pltpu.CompilerParams(
            collective_id=0, has_side_effects=True, vmem_limit_bytes=52 * 1024 * 1024
        ),
    )(
        ctx_len, entry_lender, entry_blocks, entry_slot,
        queries.transpose(1, 0, 2), new_kv.transpose(0, 2, 1, 3), key_value_pool, out_weight,
    )
    return att.transpose(1, 0, 2), proj.transpose(1, 0, 2)


def solution(mesh):
    return jax.shard_map(
        local,
        mesh=mesh,
        in_specs=(
            P("inst", None, "tp"),
            P("inst", None, None, "tp"),
            P("inst", None, None, "tp"),
            P("inst"),
            P("inst", None),
            P("inst", None),
            P("inst", None),
            P("tp", None),
        ),
        out_specs=(P("inst", None, "tp"), P("inst", None, "tp")),
        check_vma=False,
    )
```

```python
import functools
import math

import jax
import jax.numpy as jnp
from jax import lax
from jax.experimental import pallas as pl
from jax.experimental.pallas import tpu as pltpu
from jax.sharding import PartitionSpec as P

HEAD_SIZE = 128
GROUP = 8
MOST_BLOCKS = 3
MESH = pl.DeviceIdType.MESH
SCALE = 1.0 / math.sqrt(HEAD_SIZE)


def attend(q, keys, values, seen, kv_heads):
    rows = q.shape[0]
    per = rows // kv_heads
    if kv_heads > 1:
        wide = jnp.concatenate([q] * kv_heads, axis=1)
        r = lax.broadcasted_iota(jnp.int32, wide.shape, 0) // per
        c = lax.broadcasted_iota(jnp.int32, wide.shape, 1) // HEAD_SIZE
        wide = jnp.where(r == c, wide.astype(jnp.float32), 0.0).astype(jnp.bfloat16)
    else:
        wide = q
    s = lax.dot_general(wide, keys, (((1,), (1,)), ((), ())), preferred_element_type=jnp.float32) * SCALE
    s = jnp.where(seen, s, -1e30)
    top = jnp.max(s, axis=1, keepdims=True)
    e = jnp.exp(s - top)
    total = jnp.sum(e, axis=1, keepdims=True)
    o = jnp.dot(e.astype(jnp.bfloat16), values, preferred_element_type=jnp.float32)
    if kv_heads > 1:
        o = jnp.concatenate(
            [o[a * per : (a + 1) * per, a * HEAD_SIZE : (a + 1) * HEAD_SIZE] for a in range(kv_heads)], axis=0
        )
    return o * (1.0 / total), top + jnp.log(total)


def to_rows(columns):
    pad = jnp.zeros((128 - columns.shape[0], 128), columns.dtype)
    return jnp.transpose(jnp.concatenate([columns, pad], axis=0))


def kernel(
    dims,
    ctx_hbm, lender_hbm, blocks_hbm, slot_hbm, q_hbm, new_hbm, pool_hbm, weight_hbm,
    att_ref, proj_ref,
    pool, weight, ctx_ref, lender_ref, blocks_ref, slot_ref, q_ref, new_ref, got_q, send_meta, got_meta, live_smem, plan_vmem, plan, send_part, got_part, send_lse,
    got_lse, home_part, spread, attn, send_y, got_y, queries, queries_in, fresh_rows,
    pool_sem, weight_sem, q_send, q_recv, m_send, m_recv, smem_sem, p_send, p_recv, l_send, l_recv, y_send, y_recv,
    plan_sem, in_sem,
):
    n, tps, cap, requests, steps, kv, entries = dims
    rows = kv * steps * GROUP
    block_rows = pool.shape[2]
    span = MOST_BLOCKS * block_rows
    me = lax.axis_index("inst")
    tp = lax.axis_index("tp")
    chunk = weight.shape[2]
    outers = n // 2
    inner = me % 2
    partner = me + 1 - 2 * inner
    small = [
        pltpu.make_async_copy(src, dst, in_sem.at[i])
        for i, (src, dst) in enumerate(
            [(q_hbm, q_ref), (ctx_hbm, ctx_ref), (lender_hbm, lender_ref), (blocks_hbm, blocks_ref),
             (slot_hbm, slot_ref), (new_hbm, new_ref)]
        )
    ]
    for copy in small:
        copy.start()

    barrier = pltpu.get_barrier_semaphore()
    for j in range(1, n):
        pl.semaphore_signal(barrier, inc=1, device_id=((me + j) % n, tp), device_id_type=MESH)
    for o in range(1, tps):
        pl.semaphore_signal(barrier, inc=1, device_id=(me, (tp + o) % tps), device_id_type=MESH)

    pool_parts = pool_sem.shape[0]
    part = pool.shape[0] // pool_parts
    pool_copies = [
        pltpu.make_async_copy(pool_hbm.at[pl.ds(i * part, part)], pool.at[pl.ds(i * part, part)], pool_sem.at[i])
        for i in range(pool_parts)
    ]
    for copy in pool_copies:
        copy.start()
    order = [tps // 2] + [o for o in range(1, tps) if o != tps // 2] + [0]
    weight_copies = {}
    for o in order:
        col = pl.multiple_of(((tp + o) % tps) * chunk, chunk)
        weight_copies[o] = pltpu.make_async_copy(weight_hbm.at[:, pl.ds(col, chunk)], weight.at[o], weight_sem.at[o])
        weight_copies[o].start()

    small[0].wait()
    for s in range(steps):
        for h in range(kv * GROUP):
            a, g = h // GROUP, h % GROUP
            block = q_ref[s, :, h * HEAD_SIZE : (h + 1) * HEAD_SIZE].astype(jnp.float32)
            spread[pl.ds((a * steps + s) * GROUP + g, requests, stride=rows), :] = block
    for r in range(requests):
        queries[r] = spread[r * rows : (r + 1) * rows, :].astype(jnp.bfloat16)

    pl.semaphore_wait(barrier, n - 1 + tps - 1)

    def q_direct(z):
        return pltpu.make_async_remote_copy(
            src_ref=queries, dst_ref=got_q.at[z], send_sem=q_send.at[z], recv_sem=q_recv.at[z],
            device_id=((me + 2 * z) % n, tp), device_id_type=MESH,
        )

    def q_relay(z, src):
        return pltpu.make_async_remote_copy(
            src_ref=src, dst_ref=got_q.at[outers + z], send_sem=q_send.at[outers + z],
            recv_sem=q_recv.at[outers + z], device_id=(partner, tp), device_id_type=MESH,
        )

    outer_order = [outers // 2] + [z for z in range(1, outers) if z != outers // 2]
    for z in outer_order:
        q_direct(z).start()
    q_relay(0, queries).start()
    for copy in small[1:]:
        copy.wait()

    plan_row = lax.broadcasted_iota(jnp.int32, (n, 128), 0)
    plan_lane = lax.broadcasted_iota(jnp.int32, (n, 128), 1)
    table = jnp.zeros((n, 128), jnp.int32)
    used = jnp.zeros((n, 128), jnp.int32)
    ranks = jnp.zeros((n, 128), jnp.int32)
    home_codes, entry_offsets = [], []
    for r in range(requests):
        before = 0
        for e in range(entries):
            blocks = blocks_ref[r, e]
            live = jnp.clip(ctx_ref[r] - block_rows * before, 0, block_rows * blocks)
            before = before + blocks
            group = lax.div(slot_ref[r, e], MOST_BLOCKS)
            if e == 0:
                home_codes.append((group, live))
                continue
            away = lender_ref[r, e] - me
            away = jnp.where(away < 0, away + n, away)
            entry_offsets.append(away)
            code = r * 65536 + group * 256 + live
            hit = plan_row == away
            table = jnp.where(hit & (plan_lane == used), code, table)
            ranks = jnp.where(hit & (plan_lane == len(entry_offsets) - 1), jnp.minimum(used, cap - 1), ranks)
            used = used + jnp.where(hit, 1, 0)
    plan_vmem[0:n] = table
    plan_vmem[n : n + 8] = jnp.broadcast_to(jnp.sum(ranks, axis=0, keepdims=True), (8, 128))
    plan_copy = pltpu.make_async_copy(plan_vmem, plan, plan_sem)
    plan_copy.start()
    for j in range(1, n):
        send_meta[j] = jnp.broadcast_to(table[j : j + 1], (8, 128))

    def m_copy(j):
        return pltpu.make_async_remote_copy(
            src_ref=send_meta.at[j], dst_ref=got_meta.at[j], send_sem=m_send.at[j], recv_sem=m_recv.at[j],
            device_id=((me + j) % n, tp), device_id_type=MESH,
        )

    def p_copy(j):
        return pltpu.make_async_remote_copy(
            src_ref=send_part.at[j], dst_ref=got_part.at[j], send_sem=p_send.at[j], recv_sem=p_recv.at[j],
            device_id=((me + n - j) % n, tp), device_id_type=MESH,
        )

    def l_copy(j):
        return pltpu.make_async_remote_copy(
            src_ref=send_lse.at[j], dst_ref=got_lse.at[j], send_sem=l_send.at[j], recv_sem=l_recv.at[j],
            device_id=((me + n - j) % n, tp), device_id_type=MESH,
        )

    for j in range(1, n):
        m_copy(j).start()
    plan_copy.wait()
    fresh_rows[...] = jnp.zeros_like(fresh_rows)
    for r in range(requests):
        for i in range(steps):
            pair = new_ref[r, i].astype(jnp.float32)
            for c in range(2):
                fresh_rows[r, c, i : i + 1, :] = pair[c : c + 1]
    for copy in pool_copies:
        copy.wait()

    def fetch(group):
        taken = pool[pl.ds(group * MOST_BLOCKS, MOST_BLOCKS)]
        return taken[:, 0].reshape(span, kv * HEAD_SIZE), taken[:, 1].reshape(span, kv * HEAD_SIZE)

    lane = lax.broadcasted_iota(jnp.int32, (rows, 128), 1)
    fresh = fresh_rows.shape[2]
    home_col = lax.broadcasted_iota(jnp.int32, (rows, span + fresh), 1)
    home_step = (lax.broadcasted_iota(jnp.int32, (rows, span + fresh), 0) // GROUP) % steps
    own_seen = (home_col >= span) & (home_col - span <= home_step)

    home_columns = jnp.zeros((rows, 128), jnp.float32)
    for r in range(requests):
        group, live = home_codes[r]
        keys, values = fetch(group)
        keys = jnp.concatenate([keys, fresh_rows[r, 0].astype(jnp.bfloat16)], axis=0)
        values = jnp.concatenate([values, fresh_rows[r, 1].astype(jnp.bfloat16)], axis=0)
        o, lse = attend(queries[r], keys, values, (home_col < live) | own_seen, kv)
        home_part[r] = o.astype(jnp.bfloat16)
        home_columns = jnp.where(lane == r, lse, home_columns)
    home_lse = to_rows(home_columns)[:requests]

    lent_col = lax.broadcasted_iota(jnp.int32, (rows, span), 1)

    def lend(slot, j):
        m_copy(j).wait_recv()
        down = pltpu.make_async_copy(got_meta.at[j], live_smem.at[j], smem_sem.at[j])
        down.start()
        queries_in[...] = got_q[slot]
        down.wait()
        columns = jnp.zeros((rows, 128), jnp.float32)
        for k in range(cap):
            code = live_smem[j, 0, k]
            keys, values = fetch(lax.shift_right_logical(code, 8) & 255)
            q = queries_in[lax.shift_right_logical(code, 16)]
            o, lse = attend(q, keys, values, lent_col < (code & 255), kv)
            send_part[j, k] = o.astype(jnp.bfloat16)
            columns = jnp.where(lane == k, lse, columns)
        send_lse[j] = to_rows(columns)[:8]
        p_copy(j).start()
        l_copy(j).start()

    def near(i, carry):
        z = jnp.where(i == 1, outers // 2, jnp.where(i <= outers // 2, i - 1, i))
        q_direct(z).wait_recv()
        q_relay(z, got_q.at[z]).start()
        lend(z, 2 * z)
        return carry

    def relayed(i, carry):
        z = jnp.where(i == 1, outers // 2, jnp.where((i > 1) & (i <= outers // 2), i - 1, i))
        q_relay(z, queries).wait_recv()
        lend(outers + z, (2 * z - 1 + 2 * inner + n) % n)
        return carry

    relayed(0, 0)
    lax.fori_loop(1, outers, near, 0)
    lax.fori_loop(1, outers, relayed, 0)

    for j in range(1, n):
        l_copy(j).wait_recv()
    logsums = [home_lse]
    for e in range(1, entries):
        picked = []
        for r in range(requests):
            item = r * (entries - 1) + e - 1
            picked.append(got_lse[entry_offsets[item], pl.ds(plan[n, item], 1), :])
        logsums.append(jnp.concatenate(picked, axis=0))
    highest = functools.reduce(jnp.maximum, logsums)
    weights = [jnp.exp(x - highest) for x in logsums]
    inverse = 1.0 / functools.reduce(jnp.add, weights)
    stacked = jnp.concatenate([w * inverse for w in weights], axis=0)
    stacked = jnp.concatenate([stacked, jnp.zeros((128 - stacked.shape[0], 128), jnp.float32)], axis=0)
    by_head = jnp.transpose(stacked)[:rows]

    for j in range(1, n):
        p_copy(j).wait_recv()
    for r in range(requests):
        total = by_head[:, r : r + 1] * home_part[r].astype(jnp.float32)
        for e in range(1, entries):
            item = r * (entries - 1) + e - 1
            far = got_part[entry_offsets[item], plan[n, item]]
            c = e * requests + r
            total = total + by_head[:, c : c + 1] * far.astype(jnp.float32)
        spread[r * rows : (r + 1) * rows, :] = total
    tokens = requests * steps
    for h in range(kv * GROUP):
        a, g = h // GROUP, h % GROUP
        block = jnp.concatenate(
            [spread[pl.ds((a * steps + s) * GROUP + g, requests, stride=rows), :] for s in range(steps)], axis=0
        )
        attn[:, h * HEAD_SIZE : (h + 1) * HEAD_SIZE] = block.astype(jnp.bfloat16)
        for s in range(steps):
            att_ref[s, :, h * HEAD_SIZE : (h + 1) * HEAD_SIZE] = block[s * requests : (s + 1) * requests].astype(
                jnp.bfloat16
            )

    def y_copy(o):
        return pltpu.make_async_remote_copy(
            src_ref=send_y.at[o], dst_ref=got_y.at[o], send_sem=y_send.at[o], recv_sem=y_recv.at[o],
            device_id=(me, (tp + o) % tps), device_id_type=MESH,
        )

    half = chunk // 2
    own = None
    for o in order:
        weight_copies[o].wait()
        y = jnp.dot(attn[...], weight[o], preferred_element_type=jnp.float32)
        y = jnp.concatenate([y[:, :half], y[:, half:]], axis=0)
        if o == 0:
            own = y
        else:
            send_y[o] = y.astype(jnp.bfloat16)
            y_copy(o).start()
    for o in order[:-1]:
        y_copy(o).wait_recv()
        own = own + got_y[o].astype(jnp.float32)
    for s in range(steps):
        proj_ref[s, :, :half] = own[s * requests : (s + 1) * requests].astype(jnp.bfloat16)
        proj_ref[s, :, half:] = own[tokens + s * requests : tokens + (s + 1) * requests].astype(jnp.bfloat16)

    for j in range(1, n):
        m_copy(j).wait_send()
        p_copy(j).wait_send()
        l_copy(j).wait_send()
    for z in range(1, outers):
        q_direct(z).wait_send()
    for z in range(outers):
        q_relay(z, queries).wait_send()
    for o in range(1, tps):
        y_copy(o).wait_send()


def local(queries, new_kv, key_value_pool, ctx_len, entry_lender, entry_blocks, entry_slot, out_weight):
    requests, steps, query_width = queries.shape
    heads = query_width // HEAD_SIZE
    kv = key_value_pool.shape[3] // HEAD_SIZE
    entries = entry_lender.shape[1]
    n = lax.axis_size("inst")
    tps = lax.axis_size("tp")
    items = requests * (entries - 1)
    cap = 2 * ((items // 2 + n - 2) // (n - 1))
    rows = heads * steps

    tokens = requests * steps
    chunk = out_weight.shape[1] // tps
    vmem = pl.BlockSpec(memory_space=pltpu.VMEM)
    hbm = pl.BlockSpec(memory_space=pltpu.HBM)
    bf, f32 = jnp.bfloat16, jnp.float32
    dma = pltpu.SemaphoreType.DMA
    att, proj = pl.pallas_call(
        functools.partial(kernel, (n, tps, cap, requests, steps, kv, entries)),
        out_shape=(
            jax.ShapeDtypeStruct((steps, requests, query_width), bf),
            jax.ShapeDtypeStruct((steps, requests, chunk), bf),
        ),
        in_specs=[hbm] * 8,
        out_specs=(vmem, vmem),
        scratch_shapes=[
            pltpu.VMEM(key_value_pool.shape, bf),
            pltpu.VMEM((tps, out_weight.shape[0], chunk), bf),
            pltpu.SMEM(ctx_len.shape, jnp.int32),
            pltpu.SMEM(entry_lender.shape, jnp.int32),
            pltpu.SMEM(entry_lender.shape, jnp.int32),
            pltpu.SMEM(entry_lender.shape, jnp.int32),
            pltpu.VMEM((steps, requests, query_width), bf),
            pltpu.VMEM((requests, steps, 2, new_kv.shape[3]), bf),
            pltpu.VMEM((n, requests, rows, HEAD_SIZE), bf),
            pltpu.VMEM((n, 8, 128), jnp.int32),
            pltpu.VMEM((n, 8, 128), jnp.int32),
            pltpu.SMEM((n, 8, 128), jnp.int32),
            pltpu.VMEM((n + 8, 128), jnp.int32),
            pltpu.SMEM((n + 8, 128), jnp.int32),
            pltpu.VMEM((n, cap, rows, HEAD_SIZE), bf),
            pltpu.VMEM((n, cap, rows, HEAD_SIZE), bf),
            pltpu.VMEM((n, 8, 128), f32),
            pltpu.VMEM((n, 8, 128), f32),
            pltpu.VMEM((requests, rows, HEAD_SIZE), bf),
            pltpu.VMEM((requests * rows, HEAD_SIZE), f32),
            pltpu.VMEM((tokens, query_width), bf),
            pltpu.VMEM((tps, 2 * tokens, chunk // 2), bf),
            pltpu.VMEM((tps, 2 * tokens, chunk // 2), bf),
            pltpu.VMEM((requests, rows, HEAD_SIZE), bf),
            pltpu.VMEM((requests, rows, HEAD_SIZE), bf),
            pltpu.VMEM((requests, 2, 16, key_value_pool.shape[3]), f32),
            dma((4,)), dma((tps,)),
            dma((n,)), dma((n,)), dma((n,)), dma((n,)), dma((n,)),
            dma((n,)), dma((n,)), dma((n,)), dma((n,)),
            dma((tps,)), dma((tps,)), dma, dma((6,)),
        ],
        compiler_params=pltpu.CompilerParams(
            collective_id=0, has_side_effects=True, vmem_limit_bytes=64 * 1024 * 1024
        ),
    )(
        ctx_len, entry_lender, entry_blocks, entry_slot,
        queries.transpose(1, 0, 2), new_kv.transpose(0, 2, 1, 3), key_value_pool, out_weight,
    )
    return att.transpose(1, 0, 2), proj.transpose(1, 0, 2)


def solution(mesh):
    return jax.shard_map(
        local,
        mesh=mesh,
        in_specs=(
            P("inst", None, "tp"),
            P("inst", None, None, "tp"),
            P("inst", None, None, "tp"),
            P("inst"),
            P("inst", None),
            P("inst", None),
            P("inst", None),
            P("tp", None),
        ),
        out_specs=(P("inst", None, "tp"), P("inst", None, "tp")),
        check_vma=False,
    )
```

```python
import functools
import math

import jax
import jax.numpy as jnp
from jax import lax
from jax.experimental import pallas as pl
from jax.experimental.pallas import tpu as pltpu
from jax.sharding import PartitionSpec as P

HEAD_SIZE = 128
GROUP = 8
MOST_BLOCKS = 3
MESH = pl.DeviceIdType.MESH
SCALE = 1.0 / math.sqrt(HEAD_SIZE)


def attend(q, keys, values, seen, kv_heads):
    rows = q.shape[0]
    per = rows // kv_heads
    if kv_heads > 1:
        wide = jnp.concatenate([q] * kv_heads, axis=1)
        r = lax.broadcasted_iota(jnp.int32, wide.shape, 0) // per
        c = lax.broadcasted_iota(jnp.int32, wide.shape, 1) // HEAD_SIZE
        wide = jnp.where(r == c, wide.astype(jnp.float32), 0.0).astype(jnp.bfloat16)
    else:
        wide = q
    s = lax.dot_general(wide, keys, (((1,), (1,)), ((), ())), preferred_element_type=jnp.float32) * SCALE
    s = jnp.where(seen, s, -1e30)
    top = jnp.max(s, axis=1, keepdims=True)
    e = jnp.exp(s - top)
    total = jnp.sum(e, axis=1, keepdims=True)
    o = jnp.dot(e.astype(jnp.bfloat16), values, preferred_element_type=jnp.float32)
    if kv_heads > 1:
        o = jnp.concatenate(
            [o[a * per : (a + 1) * per, a * HEAD_SIZE : (a + 1) * HEAD_SIZE] for a in range(kv_heads)], axis=0
        )
    return o * (1.0 / total), top + jnp.log(total)


def to_rows(columns):
    pad = jnp.zeros((128 - columns.shape[0], 128), columns.dtype)
    return jnp.transpose(jnp.concatenate([columns, pad], axis=0))


def kernel(
    dims,
    ctx_hbm, lender_hbm, blocks_hbm, slot_hbm, q_hbm, new_hbm, pool_hbm, weight_hbm,
    att_ref, proj_ref,
    pool, weight, ctx_ref, lender_ref, blocks_ref, slot_ref, q_ref, new_ref, got_q, send_meta, got_meta, live_smem, plan_vmem, plan, send_part, got_part, send_lse,
    got_lse, home_part, spread, attn, send_y, got_y, queries, queries_in, fresh_rows,
    pool_sem, weight_sem, q_send, q_recv, m_send, m_recv, smem_sem, p_send, p_recv, l_send, l_recv, y_send, y_recv,
    plan_sem, in_sem,
):
    n, tps, cap, requests, steps, kv, entries = dims
    rows = kv * steps * GROUP
    block_rows = pool.shape[2]
    span = MOST_BLOCKS * block_rows
    me = lax.axis_index("inst")
    tp = lax.axis_index("tp")
    chunk = weight.shape[2]
    outers = n // 2
    inner = me % 2
    partner = me + 1 - 2 * inner
    small = [
        pltpu.make_async_copy(src, dst, in_sem.at[i])
        for i, (src, dst) in enumerate(
            [(q_hbm, q_ref), (ctx_hbm, ctx_ref), (lender_hbm, lender_ref), (blocks_hbm, blocks_ref),
             (slot_hbm, slot_ref), (new_hbm, new_ref)]
        )
    ]
    for copy in small:
        copy.start()

    barrier = pltpu.get_barrier_semaphore()
    for j in range(1, n):
        pl.semaphore_signal(barrier, inc=1, device_id=((me + j) % n, tp), device_id_type=MESH)
    for o in range(1, tps):
        pl.semaphore_signal(barrier, inc=1, device_id=(me, (tp + o) % tps), device_id_type=MESH)

    pool_parts = pool_sem.shape[0]
    part = pool.shape[0] // pool_parts
    pool_copies = [
        pltpu.make_async_copy(pool_hbm.at[pl.ds(i * part, part)], pool.at[pl.ds(i * part, part)], pool_sem.at[i])
        for i in range(pool_parts)
    ]
    for copy in pool_copies:
        copy.start()
    order = [tps // 2] + [o for o in range(1, tps) if o != tps // 2] + [0]
    weight_copies = {}
    for o in order:
        col = pl.multiple_of(((tp + o) % tps) * chunk, chunk)
        weight_copies[o] = pltpu.make_async_copy(weight_hbm.at[:, pl.ds(col, chunk)], weight.at[o], weight_sem.at[o])
        weight_copies[o].start()

    small[0].wait()
    for s in range(steps):
        for h in range(kv * GROUP):
            a, g = h // GROUP, h % GROUP
            block = q_ref[s, :, h * HEAD_SIZE : (h + 1) * HEAD_SIZE].astype(jnp.float32)
            spread[pl.ds((a * steps + s) * GROUP + g, requests, stride=rows), :] = block
    for r in range(requests):
        queries[r] = spread[r * rows : (r + 1) * rows, :].astype(jnp.bfloat16)

    pl.semaphore_wait(barrier, n - 1 + tps - 1)

    def q_direct(z):
        return pltpu.make_async_remote_copy(
            src_ref=queries, dst_ref=got_q.at[z], send_sem=q_send.at[z], recv_sem=q_recv.at[z],
            device_id=((me + 2 * z) % n, tp), device_id_type=MESH,
        )

    def q_relay(z, src):
        return pltpu.make_async_remote_copy(
            src_ref=src, dst_ref=got_q.at[outers + z], send_sem=q_send.at[outers + z],
            recv_sem=q_recv.at[outers + z], device_id=(partner, tp), device_id_type=MESH,
        )

    def q_forward(z):
        return pltpu.make_async_remote_copy(
            src_ref=got_q.at[z - 1], dst_ref=got_q.at[z], send_sem=q_send.at[z], recv_sem=q_recv.at[z],
            device_id=((me + 2) % n, tp), device_id_type=MESH,
        )

    for z in sorted({1, outers - 1}):
        q_direct(z).start()
    q_relay(0, queries).start()
    for copy in small[1:]:
        copy.wait()

    plan_row = lax.broadcasted_iota(jnp.int32, (n, 128), 0)
    plan_lane = lax.broadcasted_iota(jnp.int32, (n, 128), 1)
    table = jnp.zeros((n, 128), jnp.int32)
    used = jnp.zeros((n, 128), jnp.int32)
    ranks = jnp.zeros((n, 128), jnp.int32)
    home_codes, entry_offsets = [], []
    for r in range(requests):
        before = 0
        for e in range(entries):
            blocks = blocks_ref[r, e]
            live = jnp.clip(ctx_ref[r] - block_rows * before, 0, block_rows * blocks)
            before = before + blocks
            group = lax.div(slot_ref[r, e], MOST_BLOCKS)
            if e == 0:
                home_codes.append((group, live))
                continue
            away = lender_ref[r, e] - me
            away = jnp.where(away < 0, away + n, away)
            entry_offsets.append(away)
            code = r * 65536 + group * 256 + live
            hit = plan_row == away
            table = jnp.where(hit & (plan_lane == used), code, table)
            ranks = jnp.where(hit & (plan_lane == len(entry_offsets) - 1), jnp.minimum(used, cap - 1), ranks)
            used = used + jnp.where(hit, 1, 0)
    plan_vmem[0:n] = table
    plan_vmem[n : n + 8] = jnp.broadcast_to(jnp.sum(ranks, axis=0, keepdims=True), (8, 128))
    plan_copy = pltpu.make_async_copy(plan_vmem, plan, plan_sem)
    plan_copy.start()
    for j in range(1, n):
        send_meta[j] = jnp.broadcast_to(table[j : j + 1], (8, 128))

    def m_copy(j):
        return pltpu.make_async_remote_copy(
            src_ref=send_meta.at[j], dst_ref=got_meta.at[j], send_sem=m_send.at[j], recv_sem=m_recv.at[j],
            device_id=((me + j) % n, tp), device_id_type=MESH,
        )

    def p_copy(j):
        return pltpu.make_async_remote_copy(
            src_ref=send_part.at[j], dst_ref=got_part.at[j], send_sem=p_send.at[j], recv_sem=p_recv.at[j],
            device_id=((me + n - j) % n, tp), device_id_type=MESH,
        )

    def l_copy(j):
        return pltpu.make_async_remote_copy(
            src_ref=send_lse.at[j], dst_ref=got_lse.at[j], send_sem=l_send.at[j], recv_sem=l_recv.at[j],
            device_id=((me + n - j) % n, tp), device_id_type=MESH,
        )

    for j in range(1, n):
        m_copy(j).start()
    plan_copy.wait()
    fresh_rows[...] = jnp.zeros_like(fresh_rows)
    for r in range(requests):
        for i in range(steps):
            pair = new_ref[r, i].astype(jnp.float32)
            for c in range(2):
                fresh_rows[r, c, i : i + 1, :] = pair[c : c + 1]
    for copy in pool_copies:
        copy.wait()

    def fetch(group):
        taken = pool[pl.ds(group * MOST_BLOCKS, MOST_BLOCKS)]
        return taken[:, 0].reshape(span, kv * HEAD_SIZE), taken[:, 1].reshape(span, kv * HEAD_SIZE)

    lane = lax.broadcasted_iota(jnp.int32, (rows, 128), 1)
    fresh = fresh_rows.shape[2]
    home_col = lax.broadcasted_iota(jnp.int32, (rows, span + fresh), 1)
    home_step = (lax.broadcasted_iota(jnp.int32, (rows, span + fresh), 0) // GROUP) % steps
    own_seen = (home_col >= span) & (home_col - span <= home_step)

    home_columns = jnp.zeros((rows, 128), jnp.float32)
    for r in range(requests):
        group, live = home_codes[r]
        keys, values = fetch(group)
        keys = jnp.concatenate([keys, fresh_rows[r, 0].astype(jnp.bfloat16)], axis=0)
        values = jnp.concatenate([values, fresh_rows[r, 1].astype(jnp.bfloat16)], axis=0)
        o, lse = attend(queries[r], keys, values, (home_col < live) | own_seen, kv)
        home_part[r] = o.astype(jnp.bfloat16)
        home_columns = jnp.where(lane == r, lse, home_columns)
    home_lse = to_rows(home_columns)[:requests]

    lent_col = lax.broadcasted_iota(jnp.int32, (rows, span), 1)

    def lend(slot, j):
        m_copy(j).wait_recv()
        down = pltpu.make_async_copy(got_meta.at[j], live_smem.at[j], smem_sem.at[j])
        down.start()
        queries_in[...] = got_q[slot]
        down.wait()
        columns = jnp.zeros((rows, 128), jnp.float32)
        for k in range(cap):
            code = live_smem[j, 0, k]
            keys, values = fetch(lax.shift_right_logical(code, 8) & 255)
            q = queries_in[lax.shift_right_logical(code, 16)]
            o, lse = attend(q, keys, values, lent_col < (code & 255), kv)
            send_part[j, k] = o.astype(jnp.bfloat16)
            columns = jnp.where(lane == k, lse, columns)
        send_lse[j] = to_rows(columns)[:8]
        p_copy(j).start()
        l_copy(j).start()

    def near(i, carry):
        z = jnp.where(i == 1, 1, jnp.where(i == 2, outers - 1, i - 1))
        q_direct(z).wait_recv()

        @pl.when(z + 1 < outers - 1)
        def _():
            q_forward(z + 1).start()

        q_relay(z, got_q.at[z]).start()
        lend(z, 2 * z)
        return carry

    def relayed(i, carry):
        z = jnp.where(i <= 1, i, jnp.where(i == 2, outers - 1, i - 1))
        q_relay(z, queries).wait_recv()
        lend(outers + z, (2 * z - 1 + 2 * inner + n) % n)
        return carry

    relayed(0, 0)
    lax.fori_loop(1, outers, near, 0)
    lax.fori_loop(1, outers, relayed, 0)

    for j in range(1, n):
        l_copy(j).wait_recv()
    logsums = [home_lse]
    for e in range(1, entries):
        picked = []
        for r in range(requests):
            item = r * (entries - 1) + e - 1
            picked.append(got_lse[entry_offsets[item], pl.ds(plan[n, item], 1), :])
        logsums.append(jnp.concatenate(picked, axis=0))
    highest = functools.reduce(jnp.maximum, logsums)
    weights = [jnp.exp(x - highest) for x in logsums]
    inverse = 1.0 / functools.reduce(jnp.add, weights)
    stacked = jnp.concatenate([w * inverse for w in weights], axis=0)
    stacked = jnp.concatenate([stacked, jnp.zeros((128 - stacked.shape[0], 128), jnp.float32)], axis=0)
    by_head = jnp.transpose(stacked)[:rows]

    for j in range(1, n):
        p_copy(j).wait_recv()
    for r in range(requests):
        total = by_head[:, r : r + 1] * home_part[r].astype(jnp.float32)
        for e in range(1, entries):
            item = r * (entries - 1) + e - 1
            far = got_part[entry_offsets[item], plan[n, item]]
            c = e * requests + r
            total = total + by_head[:, c : c + 1] * far.astype(jnp.float32)
        spread[r * rows : (r + 1) * rows, :] = total
    tokens = requests * steps
    for h in range(kv * GROUP):
        a, g = h // GROUP, h % GROUP
        block = jnp.concatenate(
            [spread[pl.ds((a * steps + s) * GROUP + g, requests, stride=rows), :] for s in range(steps)], axis=0
        )
        attn[:, h * HEAD_SIZE : (h + 1) * HEAD_SIZE] = block.astype(jnp.bfloat16)
        for s in range(steps):
            att_ref[s, :, h * HEAD_SIZE : (h + 1) * HEAD_SIZE] = block[s * requests : (s + 1) * requests].astype(
                jnp.bfloat16
            )

    def y_copy(o):
        return pltpu.make_async_remote_copy(
            src_ref=send_y.at[o], dst_ref=got_y.at[o], send_sem=y_send.at[o], recv_sem=y_recv.at[o],
            device_id=(me, (tp + o) % tps), device_id_type=MESH,
        )

    half = chunk // 2
    own = None
    for o in order:
        weight_copies[o].wait()
        y = jnp.dot(attn[...], weight[o], preferred_element_type=jnp.float32)
        y = jnp.concatenate([y[:, :half], y[:, half:]], axis=0)
        if o == 0:
            own = y
        else:
            send_y[o] = y.astype(jnp.bfloat16)
            y_copy(o).start()
    for o in order[:-1]:
        y_copy(o).wait_recv()
        own = own + got_y[o].astype(jnp.float32)
    for s in range(steps):
        proj_ref[s, :, :half] = own[s * requests : (s + 1) * requests].astype(jnp.bfloat16)
        proj_ref[s, :, half:] = own[tokens + s * requests : tokens + (s + 1) * requests].astype(jnp.bfloat16)

    for j in range(1, n):
        m_copy(j).wait_send()
        p_copy(j).wait_send()
        l_copy(j).wait_send()
    for z in range(1, outers):
        q_direct(z).wait_send()
    for z in range(outers):
        q_relay(z, queries).wait_send()
    for o in range(1, tps):
        y_copy(o).wait_send()


def local(queries, new_kv, key_value_pool, ctx_len, entry_lender, entry_blocks, entry_slot, out_weight):
    requests, steps, query_width = queries.shape
    heads = query_width // HEAD_SIZE
    kv = key_value_pool.shape[3] // HEAD_SIZE
    entries = entry_lender.shape[1]
    n = lax.axis_size("inst")
    tps = lax.axis_size("tp")
    items = requests * (entries - 1)
    cap = 2 * ((items // 2 + n - 2) // (n - 1))
    rows = heads * steps

    tokens = requests * steps
    chunk = out_weight.shape[1] // tps
    vmem = pl.BlockSpec(memory_space=pltpu.VMEM)
    hbm = pl.BlockSpec(memory_space=pltpu.HBM)
    bf, f32 = jnp.bfloat16, jnp.float32
    dma = pltpu.SemaphoreType.DMA
    att, proj = pl.pallas_call(
        functools.partial(kernel, (n, tps, cap, requests, steps, kv, entries)),
        out_shape=(
            pltpu.VMEM((steps, requests, query_width), bf),
            pltpu.VMEM((steps, requests, chunk), bf),
        ),
        in_specs=[hbm] * 8,
        out_specs=(vmem, vmem),
        scratch_shapes=[
            pltpu.VMEM(key_value_pool.shape, bf),
            pltpu.VMEM((tps, out_weight.shape[0], chunk), bf),
            pltpu.SMEM(ctx_len.shape, jnp.int32),
            pltpu.SMEM(entry_lender.shape, jnp.int32),
            pltpu.SMEM(entry_lender.shape, jnp.int32),
            pltpu.SMEM(entry_lender.shape, jnp.int32),
            pltpu.VMEM((steps, requests, query_width), bf),
            pltpu.VMEM((requests, steps, 2, new_kv.shape[3]), bf),
            pltpu.VMEM((n, requests, rows, HEAD_SIZE), bf),
            pltpu.VMEM((n, 8, 128), jnp.int32),
            pltpu.VMEM((n, 8, 128), jnp.int32),
            pltpu.SMEM((n, 8, 128), jnp.int32),
            pltpu.VMEM((n + 8, 128), jnp.int32),
            pltpu.SMEM((n + 8, 128), jnp.int32),
            pltpu.VMEM((n, cap, rows, HEAD_SIZE), bf),
            pltpu.VMEM((n, cap, rows, HEAD_SIZE), bf),
            pltpu.VMEM((n, 8, 128), f32),
            pltpu.VMEM((n, 8, 128), f32),
            pltpu.VMEM((requests, rows, HEAD_SIZE), bf),
            pltpu.VMEM((requests * rows, HEAD_SIZE), f32),
            pltpu.VMEM((tokens, query_width), bf),
            pltpu.VMEM((tps, 2 * tokens, chunk // 2), bf),
            pltpu.VMEM((tps, 2 * tokens, chunk // 2), bf),
            pltpu.VMEM((requests, rows, HEAD_SIZE), bf),
            pltpu.VMEM((requests, rows, HEAD_SIZE), bf),
            pltpu.VMEM((requests, 2, 16, key_value_pool.shape[3]), f32),
            dma((4,)), dma((tps,)),
            dma((n,)), dma((n,)), dma((n,)), dma((n,)), dma((n,)),
            dma((n,)), dma((n,)), dma((n,)), dma((n,)),
            dma((tps,)), dma((tps,)), dma, dma((6,)),
        ],
        compiler_params=pltpu.CompilerParams(
            collective_id=0, has_side_effects=True, vmem_limit_bytes=60 * 1024 * 1024
        ),
    )(
        ctx_len, entry_lender, entry_blocks, entry_slot,
        queries.transpose(1, 0, 2), new_kv.transpose(0, 2, 1, 3), key_value_pool, out_weight,
    )
    return att.transpose(1, 0, 2), proj.transpose(1, 0, 2)


def solution(mesh):
    return jax.shard_map(
        local,
        mesh=mesh,
        in_specs=(
            P("inst", None, "tp"),
            P("inst", None, None, "tp"),
            P("inst", None, None, "tp"),
            P("inst"),
            P("inst", None),
            P("inst", None),
            P("inst", None),
            P("tp", None),
        ),
        out_specs=(P("inst", None, "tp"), P("inst", None, "tp")),
        check_vma=False,
    )
```

```python
import functools
import math

import jax
import jax.numpy as jnp
from jax import lax
from jax.experimental import pallas as pl
from jax.experimental.pallas import tpu as pltpu
from jax.sharding import PartitionSpec as P

HEAD_SIZE = 128
GROUP = 8
MOST_BLOCKS = 3
MESH = pl.DeviceIdType.MESH
SCALE = 1.0 / math.sqrt(HEAD_SIZE)


def attend(q, keys, values, seen, kv_heads):
    rows = q.shape[0]
    per = rows // kv_heads
    if kv_heads > 1:
        wide = jnp.concatenate([q] * kv_heads, axis=1)
        r = lax.broadcasted_iota(jnp.int32, wide.shape, 0) // per
        c = lax.broadcasted_iota(jnp.int32, wide.shape, 1) // HEAD_SIZE
        wide = jnp.where(r == c, wide.astype(jnp.float32), 0.0).astype(jnp.bfloat16)
    else:
        wide = q
    s = lax.dot_general(wide, keys, (((1,), (1,)), ((), ())), preferred_element_type=jnp.float32) * SCALE
    s = jnp.where(seen, s, -1e30)
    top = jnp.max(s, axis=1, keepdims=True)
    e = jnp.exp(s - top)
    total = jnp.sum(e, axis=1, keepdims=True)
    o = jnp.dot(e.astype(jnp.bfloat16), values, preferred_element_type=jnp.float32)
    if kv_heads > 1:
        o = jnp.concatenate(
            [o[a * per : (a + 1) * per, a * HEAD_SIZE : (a + 1) * HEAD_SIZE] for a in range(kv_heads)], axis=0
        )
    return o * (1.0 / total), top + jnp.log(total)


def to_rows(columns):
    pad = jnp.zeros((128 - columns.shape[0], 128), columns.dtype)
    return jnp.transpose(jnp.concatenate([columns, pad], axis=0))


def kernel(
    dims,
    ctx_hbm, lender_hbm, blocks_hbm, slot_hbm, q_hbm, new_hbm, pool_hbm, weight_hbm,
    att_ref, proj_ref,
    pool, weight, ctx_ref, lender_ref, blocks_ref, slot_ref, q_ref, new_ref, got_q, send_meta, got_meta, live_smem, plan_vmem, plan, send_part, got_part, send_lse,
    got_lse, home_part, spread, attn, send_y, got_y, queries, queries_in, fresh_rows,
    pool_sem, weight_sem, q_send, q_recv, m_send, m_recv, smem_sem, p_send, p_recv, l_send, l_recv, y_send, y_recv,
    plan_sem, in_sem,
):
    n, tps, cap, requests, steps, kv, entries = dims
    rows = kv * steps * GROUP
    block_rows = pool.shape[2]
    span = MOST_BLOCKS * block_rows
    me = lax.axis_index("inst")
    tp = lax.axis_index("tp")
    chunk = weight.shape[2]
    outers = n // 2
    inner = me % 2
    partner = me + 1 - 2 * inner
    small = [
        pltpu.make_async_copy(src, dst, in_sem.at[i])
        for i, (src, dst) in enumerate(
            [(q_hbm, q_ref), (ctx_hbm, ctx_ref), (lender_hbm, lender_ref), (blocks_hbm, blocks_ref),
             (slot_hbm, slot_ref), (new_hbm, new_ref)]
        )
    ]
    for copy in small:
        copy.start()

    barrier = pltpu.get_barrier_semaphore()
    for j in range(1, n):
        pl.semaphore_signal(barrier, inc=1, device_id=((me + j) % n, tp), device_id_type=MESH)
    for o in range(1, tps):
        pl.semaphore_signal(barrier, inc=1, device_id=(me, (tp + o) % tps), device_id_type=MESH)

    pool_parts = pool_sem.shape[0]
    part = pool.shape[0] // pool_parts
    pool_copies = [
        pltpu.make_async_copy(pool_hbm.at[pl.ds(i * part, part)], pool.at[pl.ds(i * part, part)], pool_sem.at[i])
        for i in range(pool_parts)
    ]
    for copy in pool_copies:
        copy.start()

    small[0].wait()
    for s in range(steps):
        for h in range(kv * GROUP):
            a, g = h // GROUP, h % GROUP
            block = q_ref[s, :, h * HEAD_SIZE : (h + 1) * HEAD_SIZE].astype(jnp.float32)
            spread[pl.ds((a * steps + s) * GROUP + g, requests, stride=rows), :] = block
    for r in range(requests):
        queries[r] = spread[r * rows : (r + 1) * rows, :].astype(jnp.bfloat16)

    pl.semaphore_wait(barrier, n - 1 + tps - 1)

    def q_direct(z):
        return pltpu.make_async_remote_copy(
            src_ref=queries, dst_ref=got_q.at[z], send_sem=q_send.at[z], recv_sem=q_recv.at[z],
            device_id=((me + 2 * z) % n, tp), device_id_type=MESH,
        )

    def q_relay(z, src):
        return pltpu.make_async_remote_copy(
            src_ref=src, dst_ref=got_q.at[outers + z], send_sem=q_send.at[outers + z],
            recv_sem=q_recv.at[outers + z], device_id=(partner, tp), device_id_type=MESH,
        )

    def q_forward(z):
        return pltpu.make_async_remote_copy(
            src_ref=got_q.at[z - 1], dst_ref=got_q.at[z], send_sem=q_send.at[z], recv_sem=q_recv.at[z],
            device_id=((me + 2) % n, tp), device_id_type=MESH,
        )

    def arrive(z):
        q_direct(z).wait_recv()

        @pl.when(z + 1 < outers - 1)
        def _():
            q_forward(z + 1).start()

        q_relay(z, got_q.at[z]).start()

    for z in sorted({1, outers - 1}):
        q_direct(z).start()
    q_relay(0, queries).start()
    for copy in small[1:]:
        copy.wait()

    plan_row = lax.broadcasted_iota(jnp.int32, (n, 128), 0)
    plan_lane = lax.broadcasted_iota(jnp.int32, (n, 128), 1)
    table = jnp.zeros((n, 128), jnp.int32)
    used = jnp.zeros((n, 128), jnp.int32)
    ranks = jnp.zeros((n, 128), jnp.int32)
    home_codes, entry_offsets = [], []
    for r in range(requests):
        before = 0
        for e in range(entries):
            blocks = blocks_ref[r, e]
            live = jnp.clip(ctx_ref[r] - block_rows * before, 0, block_rows * blocks)
            before = before + blocks
            group = lax.div(slot_ref[r, e], MOST_BLOCKS)
            if e == 0:
                home_codes.append((group, live))
                continue
            away = lender_ref[r, e] - me
            away = jnp.where(away < 0, away + n, away)
            entry_offsets.append(away)
            code = r * 65536 + group * 256 + live
            hit = plan_row == away
            table = jnp.where(hit & (plan_lane == used), code, table)
            ranks = jnp.where(hit & (plan_lane == len(entry_offsets) - 1), jnp.minimum(used, cap - 1), ranks)
            used = used + jnp.where(hit, 1, 0)
    plan_vmem[0:n] = table
    plan_vmem[n : n + 8] = jnp.broadcast_to(jnp.sum(ranks, axis=0, keepdims=True), (8, 128))
    plan_copy = pltpu.make_async_copy(plan_vmem, plan, plan_sem)
    plan_copy.start()
    for j in range(1, n):
        send_meta[j] = jnp.broadcast_to(table[j : j + 1], (8, 128))

    def m_copy(j):
        return pltpu.make_async_remote_copy(
            src_ref=send_meta.at[j], dst_ref=got_meta.at[j], send_sem=m_send.at[j], recv_sem=m_recv.at[j],
            device_id=((me + j) % n, tp), device_id_type=MESH,
        )

    def p_copy(j):
        return pltpu.make_async_remote_copy(
            src_ref=send_part.at[j], dst_ref=got_part.at[j], send_sem=p_send.at[j], recv_sem=p_recv.at[j],
            device_id=((me + n - j) % n, tp), device_id_type=MESH,
        )

    def l_copy(j):
        return pltpu.make_async_remote_copy(
            src_ref=send_lse.at[j], dst_ref=got_lse.at[j], send_sem=l_send.at[j], recv_sem=l_recv.at[j],
            device_id=((me + n - j) % n, tp), device_id_type=MESH,
        )

    for j in range(1, n):
        m_copy(j).start()
    plan_copy.wait()
    fresh_rows[...] = jnp.zeros_like(fresh_rows)
    for r in range(requests):
        for i in range(steps):
            pair = new_ref[r, i].astype(jnp.float32)
            for c in range(2):
                fresh_rows[r, c, i : i + 1, :] = pair[c : c + 1]
    for copy in pool_copies:
        copy.wait()
    order = [tps // 2] + [o for o in range(1, tps) if o != tps // 2] + [0]
    weight_copies = {}
    for o in order:
        col = pl.multiple_of(((tp + o) % tps) * chunk, chunk)
        weight_copies[o] = pltpu.make_async_copy(weight_hbm.at[:, pl.ds(col, chunk)], weight.at[o], weight_sem.at[o])
        weight_copies[o].start()

    def fetch(group):
        taken = pool[pl.ds(group * MOST_BLOCKS, MOST_BLOCKS)]
        return taken[:, 0].reshape(span, kv * HEAD_SIZE), taken[:, 1].reshape(span, kv * HEAD_SIZE)

    lane = lax.broadcasted_iota(jnp.int32, (rows, 128), 1)
    fresh = fresh_rows.shape[2]
    home_col = lax.broadcasted_iota(jnp.int32, (rows, span + fresh), 1)
    home_step = (lax.broadcasted_iota(jnp.int32, (rows, span + fresh), 0) // GROUP) % steps
    own_seen = (home_col >= span) & (home_col - span <= home_step)

    home_columns = jnp.zeros((rows, 128), jnp.float32)
    early = sorted({1, outers - 1})
    for r in range(requests):
        if r in (requests // 2, requests - 1):
            for z in early[:1] if r == requests // 2 else early[1:]:
                arrive(z)
        group, live = home_codes[r]
        keys, values = fetch(group)
        keys = jnp.concatenate([keys, fresh_rows[r, 0].astype(jnp.bfloat16)], axis=0)
        values = jnp.concatenate([values, fresh_rows[r, 1].astype(jnp.bfloat16)], axis=0)
        o, lse = attend(queries[r], keys, values, (home_col < live) | own_seen, kv)
        home_part[r] = o.astype(jnp.bfloat16)
        home_columns = jnp.where(lane == r, lse, home_columns)
    home_lse = to_rows(home_columns)[:requests]

    lent_col = lax.broadcasted_iota(jnp.int32, (rows, span), 1)

    def lend(slot, j):
        m_copy(j).wait_recv()
        down = pltpu.make_async_copy(got_meta.at[j], live_smem.at[j], smem_sem.at[j])
        down.start()
        queries_in[...] = got_q[slot]
        down.wait()
        columns = jnp.zeros((rows, 128), jnp.float32)
        for k in range(cap):
            code = live_smem[j, 0, k]
            keys, values = fetch(lax.shift_right_logical(code, 8) & 255)
            q = queries_in[lax.shift_right_logical(code, 16)]
            o, lse = attend(q, keys, values, lent_col < (code & 255), kv)
            send_part[j, k] = o.astype(jnp.bfloat16)
            columns = jnp.where(lane == k, lse, columns)
        send_lse[j] = to_rows(columns)[:8]
        p_copy(j).start()
        l_copy(j).start()

    def near(i, carry):
        z = jnp.where(i == 1, 1, jnp.where(i == 2, outers - 1, i - 1))

        @pl.when(i > 2)
        def _():
            arrive(z)

        lend(z, 2 * z)
        return carry

    def relayed(i, carry):
        z = jnp.where(i <= 1, i, jnp.where(i == 2, outers - 1, i - 1))
        q_relay(z, queries).wait_recv()
        lend(outers + z, (2 * z - 1 + 2 * inner + n) % n)
        return carry

    relayed(0, 0)
    lax.fori_loop(1, outers, near, 0)
    lax.fori_loop(1, outers, relayed, 0)

    for j in range(1, n):
        l_copy(j).wait_recv()
    logsums = [home_lse]
    for e in range(1, entries):
        picked = []
        for r in range(requests):
            item = r * (entries - 1) + e - 1
            picked.append(got_lse[entry_offsets[item], pl.ds(plan[n, item], 1), :])
        logsums.append(jnp.concatenate(picked, axis=0))
    highest = functools.reduce(jnp.maximum, logsums)
    weights = [jnp.exp(x - highest) for x in logsums]
    inverse = 1.0 / functools.reduce(jnp.add, weights)
    stacked = jnp.concatenate([w * inverse for w in weights], axis=0)
    stacked = jnp.concatenate([stacked, jnp.zeros((128 - stacked.shape[0], 128), jnp.float32)], axis=0)
    by_head = jnp.transpose(stacked)[:rows]

    for j in range(1, n):
        p_copy(j).wait_recv()
    for r in range(requests):
        total = by_head[:, r : r + 1] * home_part[r].astype(jnp.float32)
        for e in range(1, entries):
            item = r * (entries - 1) + e - 1
            far = got_part[entry_offsets[item], plan[n, item]]
            c = e * requests + r
            total = total + by_head[:, c : c + 1] * far.astype(jnp.float32)
        spread[r * rows : (r + 1) * rows, :] = total
    tokens = requests * steps
    for h in range(kv * GROUP):
        a, g = h // GROUP, h % GROUP
        block = jnp.concatenate(
            [spread[pl.ds((a * steps + s) * GROUP + g, requests, stride=rows), :] for s in range(steps)], axis=0
        )
        attn[:, h * HEAD_SIZE : (h + 1) * HEAD_SIZE] = block.astype(jnp.bfloat16)
        for s in range(steps):
            att_ref[s, :, h * HEAD_SIZE : (h + 1) * HEAD_SIZE] = block[s * requests : (s + 1) * requests].astype(
                jnp.bfloat16
            )

    def y_copy(o):
        return pltpu.make_async_remote_copy(
            src_ref=send_y.at[o], dst_ref=got_y.at[o], send_sem=y_send.at[o], recv_sem=y_recv.at[o],
            device_id=(me, (tp + o) % tps), device_id_type=MESH,
        )

    half = chunk // 2
    own = None
    for o in order:
        weight_copies[o].wait()
        y = jnp.dot(attn[...], weight[o], preferred_element_type=jnp.float32)
        y = jnp.concatenate([y[:, :half], y[:, half:]], axis=0)
        if o == 0:
            own = y
        else:
            send_y[o] = y.astype(jnp.bfloat16)
            y_copy(o).start()
    for o in order[:-1]:
        y_copy(o).wait_recv()
        own = own + got_y[o].astype(jnp.float32)
    for s in range(steps):
        proj_ref[s, :, :half] = own[s * requests : (s + 1) * requests].astype(jnp.bfloat16)
        proj_ref[s, :, half:] = own[tokens + s * requests : tokens + (s + 1) * requests].astype(jnp.bfloat16)

    for j in range(1, n):
        m_copy(j).wait_send()
        p_copy(j).wait_send()
        l_copy(j).wait_send()
    for z in range(1, outers):
        q_direct(z).wait_send()
    for z in range(outers):
        q_relay(z, queries).wait_send()
    for o in range(1, tps):
        y_copy(o).wait_send()


def local(queries, new_kv, key_value_pool, ctx_len, entry_lender, entry_blocks, entry_slot, out_weight):
    requests, steps, query_width = queries.shape
    heads = query_width // HEAD_SIZE
    kv = key_value_pool.shape[3] // HEAD_SIZE
    entries = entry_lender.shape[1]
    n = lax.axis_size("inst")
    tps = lax.axis_size("tp")
    items = requests * (entries - 1)
    cap = 2 * ((items // 2 + n - 2) // (n - 1))
    rows = heads * steps

    tokens = requests * steps
    chunk = out_weight.shape[1] // tps
    vmem = pl.BlockSpec(memory_space=pltpu.VMEM)
    hbm = pl.BlockSpec(memory_space=pltpu.HBM)
    bf, f32 = jnp.bfloat16, jnp.float32
    dma = pltpu.SemaphoreType.DMA
    att, proj = pl.pallas_call(
        functools.partial(kernel, (n, tps, cap, requests, steps, kv, entries)),
        out_shape=(
            pltpu.VMEM((steps, requests, query_width), bf),
            pltpu.VMEM((steps, requests, chunk), bf),
        ),
        in_specs=[hbm] * 8,
        out_specs=(vmem, vmem),
        scratch_shapes=[
            pltpu.VMEM(key_value_pool.shape, bf),
            pltpu.VMEM((tps, out_weight.shape[0], chunk), bf),
            pltpu.SMEM(ctx_len.shape, jnp.int32),
            pltpu.SMEM(entry_lender.shape, jnp.int32),
            pltpu.SMEM(entry_lender.shape, jnp.int32),
            pltpu.SMEM(entry_lender.shape, jnp.int32),
            pltpu.VMEM((steps, requests, query_width), bf),
            pltpu.VMEM((requests, steps, 2, new_kv.shape[3]), bf),
            pltpu.VMEM((n, requests, rows, HEAD_SIZE), bf),
            pltpu.VMEM((n, 8, 128), jnp.int32),
            pltpu.VMEM((n, 8, 128), jnp.int32),
            pltpu.SMEM((n, 8, 128), jnp.int32),
            pltpu.VMEM((n + 8, 128), jnp.int32),
            pltpu.SMEM((n + 8, 128), jnp.int32),
            pltpu.VMEM((n, cap, rows, HEAD_SIZE), bf),
            pltpu.VMEM((n, cap, rows, HEAD_SIZE), bf),
            pltpu.VMEM((n, 8, 128), f32),
            pltpu.VMEM((n, 8, 128), f32),
            pltpu.VMEM((requests, rows, HEAD_SIZE), bf),
            pltpu.VMEM((requests * rows, HEAD_SIZE), f32),
            pltpu.VMEM((tokens, query_width), bf),
            pltpu.VMEM((tps, 2 * tokens, chunk // 2), bf),
            pltpu.VMEM((tps, 2 * tokens, chunk // 2), bf),
            pltpu.VMEM((requests, rows, HEAD_SIZE), bf),
            pltpu.VMEM((requests, rows, HEAD_SIZE), bf),
            pltpu.VMEM((requests, 2, 16, key_value_pool.shape[3]), f32),
            dma((4,)), dma((tps,)),
            dma((n,)), dma((n,)), dma((n,)), dma((n,)), dma((n,)),
            dma((n,)), dma((n,)), dma((n,)), dma((n,)),
            dma((tps,)), dma((tps,)), dma, dma((6,)),
        ],
        compiler_params=pltpu.CompilerParams(
            collective_id=0, has_side_effects=True, vmem_limit_bytes=60 * 1024 * 1024
        ),
    )(
        ctx_len, entry_lender, entry_blocks, entry_slot,
        queries.transpose(1, 0, 2), new_kv.transpose(0, 2, 1, 3), key_value_pool, out_weight,
    )
    return att.transpose(1, 0, 2), proj.transpose(1, 0, 2)


def solution(mesh):
    return jax.shard_map(
        local,
        mesh=mesh,
        in_specs=(
            P("inst", None, "tp"),
            P("inst", None, None, "tp"),
            P("inst", None, None, "tp"),
            P("inst"),
            P("inst", None),
            P("inst", None),
            P("inst", None),
            P("tp", None),
        ),
        out_specs=(P("inst", None, "tp"), P("inst", None, "tp")),
        check_vma=False,
    )
```

```python
import functools
import math

import jax
import jax.numpy as jnp
from jax import lax
from jax.experimental import pallas as pl
from jax.experimental.pallas import tpu as pltpu
from jax.sharding import PartitionSpec as P

HEAD_SIZE = 128
GROUP = 8
MOST_BLOCKS = 3
MESH = pl.DeviceIdType.MESH
SCALE = 1.0 / math.sqrt(HEAD_SIZE)


def attend(q, keys, values, seen, kv_heads):
    rows = q.shape[0]
    per = rows // kv_heads
    if kv_heads > 1:
        wide = jnp.concatenate([q] * kv_heads, axis=1)
        r = lax.broadcasted_iota(jnp.int32, wide.shape, 0) // per
        c = lax.broadcasted_iota(jnp.int32, wide.shape, 1) // HEAD_SIZE
        wide = jnp.where(r == c, wide.astype(jnp.float32), 0.0).astype(jnp.bfloat16)
    else:
        wide = q
    s = lax.dot_general(wide, keys, (((1,), (1,)), ((), ())), preferred_element_type=jnp.float32) * SCALE
    s = jnp.where(seen, s, -1e30)
    top = jnp.max(s, axis=1, keepdims=True)
    e = jnp.exp(s - top)
    total = jnp.sum(e, axis=1, keepdims=True)
    o = jnp.dot(e.astype(jnp.bfloat16), values, preferred_element_type=jnp.float32)
    if kv_heads > 1:
        o = jnp.concatenate(
            [o[a * per : (a + 1) * per, a * HEAD_SIZE : (a + 1) * HEAD_SIZE] for a in range(kv_heads)], axis=0
        )
    return o * (1.0 / total), top + jnp.log(total)


def to_rows(columns):
    pad = jnp.zeros((128 - columns.shape[0], 128), columns.dtype)
    return jnp.transpose(jnp.concatenate([columns, pad], axis=0))


def kernel(
    dims,
    ctx_hbm, lender_hbm, blocks_hbm, slot_hbm, q_hbm, new_hbm, pool_hbm, weight_hbm,
    att_ref, proj_ref,
    pool, weight, ctx_ref, lender_ref, blocks_ref, slot_ref, q_ref, new_ref, got_q, send_meta, got_meta, live_smem, plan_vmem, plan, send_part, got_part, send_lse,
    got_lse, home_part, spread, attn, send_y, got_y, queries, queries_in, fresh_rows,
    pool_sem, weight_sem, q_send, q_recv, m_send, m_recv, smem_sem, p_send, p_recv, l_send, l_recv, y_send, y_recv,
    plan_sem, in_sem,
):
    n, tps, cap, requests, steps, kv, entries = dims
    rows = kv * steps * GROUP
    block_rows = pool.shape[2]
    span = MOST_BLOCKS * block_rows
    me = lax.axis_index("inst")
    tp = lax.axis_index("tp")
    chunk = weight.shape[2]
    outers = n // 2
    inner = me % 2
    partner = me + 1 - 2 * inner
    small = [
        pltpu.make_async_copy(src, dst, in_sem.at[i])
        for i, (src, dst) in enumerate(
            [(q_hbm, q_ref), (ctx_hbm, ctx_ref), (lender_hbm, lender_ref), (blocks_hbm, blocks_ref),
             (slot_hbm, slot_ref), (new_hbm, new_ref)]
        )
    ]
    for copy in small:
        copy.start()

    barrier = pltpu.get_barrier_semaphore()
    for j in range(1, n):
        pl.semaphore_signal(barrier, inc=1, device_id=((me + j) % n, tp), device_id_type=MESH)
    for o in range(1, tps):
        pl.semaphore_signal(barrier, inc=1, device_id=(me, (tp + o) % tps), device_id_type=MESH)

    pool_parts = pool_sem.shape[0]
    part = pool.shape[0] // pool_parts
    pool_copies = [
        pltpu.make_async_copy(pool_hbm.at[pl.ds(i * part, part)], pool.at[pl.ds(i * part, part)], pool_sem.at[i])
        for i in range(pool_parts)
    ]
    for copy in pool_copies:
        copy.start()

    small[0].wait()
    for s in range(steps):
        for h in range(kv * GROUP):
            a, g = h // GROUP, h % GROUP
            block = q_ref[s, :, h * HEAD_SIZE : (h + 1) * HEAD_SIZE].astype(jnp.float32)
            spread[pl.ds((a * steps + s) * GROUP + g, requests, stride=rows), :] = block
    for r in range(requests):
        queries[r] = spread[r * rows : (r + 1) * rows, :].astype(jnp.bfloat16)

    pl.semaphore_wait(barrier, n - 1 + tps - 1)

    def q_direct(z):
        return pltpu.make_async_remote_copy(
            src_ref=queries, dst_ref=got_q.at[z], send_sem=q_send.at[z], recv_sem=q_recv.at[z],
            device_id=((me + 2 * z) % n, tp), device_id_type=MESH,
        )

    def q_relay(z, src):
        return pltpu.make_async_remote_copy(
            src_ref=src, dst_ref=got_q.at[outers + z], send_sem=q_send.at[outers + z],
            recv_sem=q_recv.at[outers + z], device_id=(partner, tp), device_id_type=MESH,
        )

    def q_forward(z):
        return pltpu.make_async_remote_copy(
            src_ref=got_q.at[z - 1], dst_ref=got_q.at[z], send_sem=q_send.at[z], recv_sem=q_recv.at[z],
            device_id=((me + 2) % n, tp), device_id_type=MESH,
        )

    def arrive(z):
        q_direct(z).wait_recv()

        @pl.when(z + 1 < outers - 1)
        def _():
            q_forward(z + 1).start()

        q_relay(z, got_q.at[z]).start()

    for z in sorted({1, outers - 1}):
        q_direct(z).start()
    q_relay(0, queries).start()
    for copy in small[1:]:
        copy.wait()

    plan_row = lax.broadcasted_iota(jnp.int32, (n, 128), 0)
    plan_lane = lax.broadcasted_iota(jnp.int32, (n, 128), 1)
    table = jnp.zeros((n, 128), jnp.int32)
    used = jnp.zeros((n, 128), jnp.int32)
    ranks = jnp.zeros((n, 128), jnp.int32)
    home_codes, entry_offsets = [], []
    for r in range(requests):
        before = 0
        for e in range(entries):
            blocks = blocks_ref[r, e]
            live = jnp.clip(ctx_ref[r] - block_rows * before, 0, block_rows * blocks)
            before = before + blocks
            group = lax.div(slot_ref[r, e], MOST_BLOCKS)
            if e == 0:
                home_codes.append((group, live))
                continue
            away = lender_ref[r, e] - me
            away = jnp.where(away < 0, away + n, away)
            entry_offsets.append(away)
            code = r * 65536 + group * 256 + live
            hit = plan_row == away
            table = jnp.where(hit & (plan_lane == used), code, table)
            ranks = jnp.where(hit & (plan_lane == len(entry_offsets) - 1), jnp.minimum(used, cap - 1), ranks)
            used = used + jnp.where(hit, 1, 0)
    plan_vmem[0:n] = table
    plan_vmem[n : n + 8] = jnp.broadcast_to(jnp.sum(ranks, axis=0, keepdims=True), (8, 128))
    plan_copy = pltpu.make_async_copy(plan_vmem, plan, plan_sem)
    plan_copy.start()
    for j in range(1, n):
        send_meta[j] = jnp.broadcast_to(table[j : j + 1], (8, 128))

    def m_copy(j):
        return pltpu.make_async_remote_copy(
            src_ref=send_meta.at[j], dst_ref=got_meta.at[j], send_sem=m_send.at[j], recv_sem=m_recv.at[j],
            device_id=((me + j) % n, tp), device_id_type=MESH,
        )

    def p_copy(j):
        return pltpu.make_async_remote_copy(
            src_ref=send_part.at[j], dst_ref=got_part.at[j], send_sem=p_send.at[j], recv_sem=p_recv.at[j],
            device_id=((me + n - j) % n, tp), device_id_type=MESH,
        )

    def l_copy(j):
        return pltpu.make_async_remote_copy(
            src_ref=send_lse.at[j], dst_ref=got_lse.at[j], send_sem=l_send.at[j], recv_sem=l_recv.at[j],
            device_id=((me + n - j) % n, tp), device_id_type=MESH,
        )

    for j in range(1, n):
        m_copy(j).start()
    plan_copy.wait()
    fresh_rows[...] = jnp.zeros_like(fresh_rows)
    for r in range(requests):
        for i in range(steps):
            pair = new_ref[r, i].astype(jnp.float32)
            for c in range(2):
                fresh_rows[r, c, i : i + 1, :] = pair[c : c + 1]
    for copy in pool_copies:
        copy.wait()
    order = [tps // 2] + [o for o in range(1, tps) if o != tps // 2] + [0]
    weight_copies = {}
    for o in order:
        col = pl.multiple_of(((tp + o) % tps) * chunk, chunk)
        weight_copies[o] = pltpu.make_async_copy(weight_hbm.at[:, pl.ds(col, chunk)], weight.at[o], weight_sem.at[o])
        weight_copies[o].start()

    def fetch(group):
        taken = pool[pl.ds(group * MOST_BLOCKS, MOST_BLOCKS)]
        return taken[:, 0].reshape(span, kv * HEAD_SIZE), taken[:, 1].reshape(span, kv * HEAD_SIZE)

    lane = lax.broadcasted_iota(jnp.int32, (rows, 128), 1)
    fresh = fresh_rows.shape[2]
    home_col = lax.broadcasted_iota(jnp.int32, (rows, span + fresh), 1)
    home_step = (lax.broadcasted_iota(jnp.int32, (rows, span + fresh), 0) // GROUP) % steps
    own_seen = (home_col >= span) & (home_col - span <= home_step)

    home_columns = jnp.zeros((rows, 128), jnp.float32)
    early = sorted({1, outers - 1})
    for r in range(requests):
        if r in (requests // 2, requests - 1):
            for z in early[:1] if r == requests // 2 else early[1:]:
                arrive(z)
        group, live = home_codes[r]
        keys, values = fetch(group)
        keys = jnp.concatenate([keys, fresh_rows[r, 0].astype(jnp.bfloat16)], axis=0)
        values = jnp.concatenate([values, fresh_rows[r, 1].astype(jnp.bfloat16)], axis=0)
        o, lse = attend(queries[r], keys, values, (home_col < live) | own_seen, kv)
        home_part[r] = o.astype(jnp.bfloat16)
        home_columns = jnp.where(lane == r, lse, home_columns)
    downs = [pltpu.make_async_copy(got_meta.at[j], live_smem.at[j], smem_sem.at[j]) for j in range(1, n)]
    for j in range(1, n):
        m_copy(j).wait_recv()
        downs[j - 1].start()
    home_lse = to_rows(home_columns)[:requests]
    for down in downs:
        down.wait()

    lent_col = lax.broadcasted_iota(jnp.int32, (rows, span), 1)

    def lend(slot, j):
        queries_in[...] = got_q[slot]
        columns = jnp.zeros((rows, 128), jnp.float32)
        for k in range(cap):
            code = live_smem[j, 0, k]
            keys, values = fetch(lax.shift_right_logical(code, 8) & 255)
            q = queries_in[lax.shift_right_logical(code, 16)]
            o, lse = attend(q, keys, values, lent_col < (code & 255), kv)
            send_part[j, k] = o.astype(jnp.bfloat16)
            columns = jnp.where(lane == k, lse, columns)
        send_lse[j] = to_rows(columns)[:8]
        l_copy(j).start()
        p_copy(j).start()

    def near(i, carry):
        z = jnp.where(i == 1, 1, jnp.where(i == 2, outers - 1, i - 1))

        @pl.when(i > 2)
        def _():
            arrive(z)

        lend(z, 2 * z)
        return carry

    def relayed(i, carry):
        z = jnp.where(i <= 1, i, jnp.where(i == 2, outers - 1, i - 1))
        q_relay(z, queries).wait_recv()
        lend(outers + z, (2 * z - 1 + 2 * inner + n) % n)
        return carry

    relayed(0, 0)
    lax.fori_loop(1, outers, near, 0)
    lax.fori_loop(1, outers, relayed, 0)

    for j in range(1, n):
        l_copy(j).wait_recv()
    logsums = [home_lse]
    for e in range(1, entries):
        picked = []
        for r in range(requests):
            item = r * (entries - 1) + e - 1
            picked.append(got_lse[entry_offsets[item], pl.ds(plan[n, item], 1), :])
        logsums.append(jnp.concatenate(picked, axis=0))
    highest = functools.reduce(jnp.maximum, logsums)
    weights = [jnp.exp(x - highest) for x in logsums]
    inverse = 1.0 / functools.reduce(jnp.add, weights)
    stacked = jnp.concatenate([w * inverse for w in weights], axis=0)
    stacked = jnp.concatenate([stacked, jnp.zeros((128 - stacked.shape[0], 128), jnp.float32)], axis=0)
    by_head = jnp.transpose(stacked)[:rows]

    for j in range(1, n):
        p_copy(j).wait_recv()
    for r in range(requests):
        total = by_head[:, r : r + 1] * home_part[r].astype(jnp.float32)
        for e in range(1, entries):
            item = r * (entries - 1) + e - 1
            far = got_part[entry_offsets[item], plan[n, item]]
            c = e * requests + r
            total = total + by_head[:, c : c + 1] * far.astype(jnp.float32)
        spread[r * rows : (r + 1) * rows, :] = total
    tokens = requests * steps
    for h in range(kv * GROUP):
        a, g = h // GROUP, h % GROUP
        block = jnp.concatenate(
            [spread[pl.ds((a * steps + s) * GROUP + g, requests, stride=rows), :] for s in range(steps)], axis=0
        )
        attn[:, h * HEAD_SIZE : (h + 1) * HEAD_SIZE] = block.astype(jnp.bfloat16)
        for s in range(steps):
            att_ref[s, :, h * HEAD_SIZE : (h + 1) * HEAD_SIZE] = block[s * requests : (s + 1) * requests].astype(
                jnp.bfloat16
            )

    def y_copy(o):
        return pltpu.make_async_remote_copy(
            src_ref=send_y.at[o], dst_ref=got_y.at[o], send_sem=y_send.at[o], recv_sem=y_recv.at[o],
            device_id=(me, (tp + o) % tps), device_id_type=MESH,
        )

    half = chunk // 2
    own = None
    for o in order:
        weight_copies[o].wait()
        y = jnp.dot(attn[...], weight[o], preferred_element_type=jnp.float32)
        y = jnp.concatenate([y[:, :half], y[:, half:]], axis=0)
        if o == 0:
            own = y
        else:
            send_y[o] = y.astype(jnp.bfloat16)
            y_copy(o).start()
    for o in order[:-1]:
        y_copy(o).wait_recv()
        own = own + got_y[o].astype(jnp.float32)
    for s in range(steps):
        proj_ref[s, :, :half] = own[s * requests : (s + 1) * requests].astype(jnp.bfloat16)
        proj_ref[s, :, half:] = own[tokens + s * requests : tokens + (s + 1) * requests].astype(jnp.bfloat16)

    for j in range(1, n):
        m_copy(j).wait_send()
        p_copy(j).wait_send()
        l_copy(j).wait_send()
    for z in range(1, outers):
        q_direct(z).wait_send()
    for z in range(outers):
        q_relay(z, queries).wait_send()
    for o in range(1, tps):
        y_copy(o).wait_send()


def local(queries, new_kv, key_value_pool, ctx_len, entry_lender, entry_blocks, entry_slot, out_weight):
    requests, steps, query_width = queries.shape
    heads = query_width // HEAD_SIZE
    kv = key_value_pool.shape[3] // HEAD_SIZE
    entries = entry_lender.shape[1]
    n = lax.axis_size("inst")
    tps = lax.axis_size("tp")
    items = requests * (entries - 1)
    cap = 2 * ((items // 2 + n - 2) // (n - 1))
    rows = heads * steps

    tokens = requests * steps
    chunk = out_weight.shape[1] // tps
    vmem = pl.BlockSpec(memory_space=pltpu.VMEM)
    hbm = pl.BlockSpec(memory_space=pltpu.HBM)
    bf, f32 = jnp.bfloat16, jnp.float32
    dma = pltpu.SemaphoreType.DMA
    att, proj = pl.pallas_call(
        functools.partial(kernel, (n, tps, cap, requests, steps, kv, entries)),
        out_shape=(
            pltpu.VMEM((steps, requests, query_width), bf),
            pltpu.VMEM((steps, requests, chunk), bf),
        ),
        in_specs=[hbm] * 8,
        out_specs=(vmem, vmem),
        scratch_shapes=[
            pltpu.VMEM(key_value_pool.shape, bf),
            pltpu.VMEM((tps, out_weight.shape[0], chunk), bf),
            pltpu.SMEM(ctx_len.shape, jnp.int32),
            pltpu.SMEM(entry_lender.shape, jnp.int32),
            pltpu.SMEM(entry_lender.shape, jnp.int32),
            pltpu.SMEM(entry_lender.shape, jnp.int32),
            pltpu.VMEM((steps, requests, query_width), bf),
            pltpu.VMEM((requests, steps, 2, new_kv.shape[3]), bf),
            pltpu.VMEM((n, requests, rows, HEAD_SIZE), bf),
            pltpu.VMEM((n, 8, 128), jnp.int32),
            pltpu.VMEM((n, 8, 128), jnp.int32),
            pltpu.SMEM((n, 8, 128), jnp.int32),
            pltpu.VMEM((n + 8, 128), jnp.int32),
            pltpu.SMEM((n + 8, 128), jnp.int32),
            pltpu.VMEM((n, cap, rows, HEAD_SIZE), bf),
            pltpu.VMEM((n, cap, rows, HEAD_SIZE), bf),
            pltpu.VMEM((n, 8, 128), f32),
            pltpu.VMEM((n, 8, 128), f32),
            pltpu.VMEM((requests, rows, HEAD_SIZE), bf),
            pltpu.VMEM((requests * rows, HEAD_SIZE), f32),
            pltpu.VMEM((tokens, query_width), bf),
            pltpu.VMEM((tps, 2 * tokens, chunk // 2), bf),
            pltpu.VMEM((tps, 2 * tokens, chunk // 2), bf),
            pltpu.VMEM((requests, rows, HEAD_SIZE), bf),
            pltpu.VMEM((requests, rows, HEAD_SIZE), bf),
            pltpu.VMEM((requests, 2, 16, key_value_pool.shape[3]), f32),
            dma((4,)), dma((tps,)),
            dma((n,)), dma((n,)), dma((n,)), dma((n,)), dma((n,)),
            dma((n,)), dma((n,)), dma((n,)), dma((n,)),
            dma((tps,)), dma((tps,)), dma, dma((6,)),
        ],
        compiler_params=pltpu.CompilerParams(
            collective_id=0, has_side_effects=True, vmem_limit_bytes=60 * 1024 * 1024
        ),
    )(
        ctx_len, entry_lender, entry_blocks, entry_slot,
        queries.transpose(1, 0, 2), new_kv.transpose(0, 2, 1, 3), key_value_pool, out_weight,
    )
    return att.transpose(1, 0, 2), proj.transpose(1, 0, 2)


def solution(mesh):
    return jax.shard_map(
        local,
        mesh=mesh,
        in_specs=(
            P("inst", None, "tp"),
            P("inst", None, None, "tp"),
            P("inst", None, None, "tp"),
            P("inst"),
            P("inst", None),
            P("inst", None),
            P("inst", None),
            P("tp", None),
        ),
        out_specs=(P("inst", None, "tp"), P("inst", None, "tp")),
        check_vma=False,
    )
```
